128 devices in a mesh: row: 16 (over x, y), col: 8 (over z, core).
Axes of the slice: x: 4, y: 4, z: 4, core: 2. Of those that a mesh axis runs over, the one named last changes fastest.
Arguments:
- object_field: float32 [2, 4096, 4096], P(None, 'row', 'col'), may hold values from -5 to 5
- probe: float32 [3, 2, 256, 256], replicated, may hold values from -6 to 6
- corners: int32 [2, 16, 8, 2, 2], P(None, 'row', 'col'), may hold values from 0 to 3840, as said below
- counts: int32 [2, 16, 8], P(None, 'row', 'col'), may hold values from 1 to 2, as said below
- amplitude: bfloat16 [2, 16, 8, 2, 256, 256], P(None, 'row', 'col'), may hold values from 0.19921875 to 4
Outputs:
- object_out: float32 [2, 4096, 4096], P(None, 'row', 'col')
- probe_out: float32 [3, 2, 256, 256], replicated
- losses: float32 [2, 16, 8], P(None, 'row', 'col')
The draws below stay inside these ranges and needn't reach their ends.
Inputs may be any that keep to these rules, and one draw needn't show every extreme that they name: corners[t, i, j, s] lies inside tile (i, j), i.e. its row in i * 256 to (i + 1) * 256 - 1 and its column in j * 512 to (j + 1) * 512 - 1, and the whole window lies inside the object of 4096 x 4096 pixels, so a window reaches at most into the tiles below, to the right and diagonally below right; in every iteration slot 0 of the first tile has corner (0, 0) and slot 0 of the last tile has corner (3840, 3840). Slots 0 to counts - 1 of a tile are live, the rest are ignored; in every iteration some tile has all 2 slots live.
All inputs are finite; a program needn't handle non-finite values.
Results may differ from the reference program's by a relative error of at most 0.0003.
Values sent between devices are 32-bit elements; how exact they have to be, the bound alone decides.
No kernel may reach another device: no remote copies, remote signals or barrier semaphores. Data moves between devices by JAX's collectives and lax.ppermute only.
A program may use at most 128 MiB of HBM per device.

```python
import math
import jax
import jax.numpy as jnp
from jax import lax

WIN = 256
MODES = 3
TR = 256
TC = 512
CAP = 2
ITERS = 2
NR = 4096
NC = 4096
N_ROW = 16
N_COL = 8


def draw_counts(key, part):
    key_busy, key_base, key_pick = jax.random.split(jax.random.fold_in(key, 11), 3)
    shape = (ITERS, N_ROW, N_COL)
    busy = jax.random.randint(key_busy, shape, 0, 20) < 3
    base = jax.random.randint(key_base, shape, 1, CAP // 2 + 1)
    chosen = jax.random.randint(key_pick, (ITERS, 1, 1), 0, N_ROW * N_COL)
    flat_tile = lax.broadcasted_iota(jnp.int32, shape, 1) * N_COL + lax.broadcasted_iota(jnp.int32, shape, 2)
    filled = jnp.where(busy | (flat_tile == chosen), CAP, base)
    return filled.astype(jnp.int32)


def draw_corners(key, part):
    key_rows, key_cols = jax.random.split(jax.random.fold_in(key, 23), 2)
    shape = (ITERS, N_ROW, N_COL, CAP)
    tile_rows = lax.broadcasted_iota(jnp.int32, shape, 1)
    tile_cols = lax.broadcasted_iota(jnp.int32, shape, 2)
    slot_index = lax.broadcasted_iota(jnp.int32, shape, 3)
    top_rows = jnp.where(tile_rows == N_ROW - 1, TR - WIN + 1, TR)
    top_cols = jnp.where(tile_cols == N_COL - 1, TC - WIN + 1, TC)
    local_rows = jax.random.randint(key_rows, shape, 0, top_rows)
    local_cols = jax.random.randint(key_cols, shape, 0, top_cols)
    first_tile = (tile_rows == 0) & (tile_cols == 0) & (slot_index == 0)
    last_tile = (tile_rows == N_ROW - 1) & (tile_cols == N_COL - 1) & (slot_index == 0)
    local_rows = jnp.where(first_tile, 0, jnp.where(last_tile, TR - WIN, local_rows))
    local_cols = jnp.where(first_tile, 0, jnp.where(last_tile, TC - WIN, local_cols))
    global_pos = jnp.stack([tile_rows * TR + local_rows, tile_cols * TC + local_cols], axis=-1)
    return global_pos.astype(jnp.int32)


def block_scale(rng, dims, pieces, smallest, top_value):
    level, own = 1.0, jax.random.fold_in(rng, 6)
    for axis_at, blocks in pieces:
        steps = jnp.exp(jax.random.uniform(jax.random.fold_in(own, axis_at), (blocks,), jnp.float32, smallest / len(pieces), top_value / len(pieces)))
        level = level * jnp.repeat(steps, dims[axis_at] // blocks).reshape([-1 if axis == axis_at else 1 for axis in range(len(dims))])
    return level


def gaussian(rng, extent, spread, bound, cuts=(), kind=jnp.bfloat16):
    factor_of = block_scale(rng, extent, cuts, -0.22, 0.18) if cuts else 1.0
    drawn = jax.random.normal(rng, extent, jnp.float32) * spread * factor_of
    return jnp.minimum(jnp.maximum(drawn, -bound), bound).astype(kind)


def setup_inputs(seed: int = 0) -> dict:
    streams_of = jax.random.split(jax.random.key(seed), 6)
    object_field = gaussian(streams_of[0], (2, NR, NC), 0.7, 5.0, ((1, 16), (2, 8)), jnp.float32)
    probe = gaussian(streams_of[1], (MODES, 2, WIN, WIN), 1.0, 6.0, (), jnp.float32)
    corners = draw_corners(jax.random.fold_in(streams_of[5], 71), 0)
    counts = draw_counts(jax.random.fold_in(streams_of[5], 71), 0)
    amplitude = jnp.clip(jnp.exp(math.log(4.0) - 2.9996462 * jax.random.uniform(streams_of[4], (ITERS, N_ROW, N_COL, CAP, WIN, WIN), jnp.float32) ** block_scale(streams_of[4], (ITERS, N_ROW, N_COL, CAP, WIN, WIN), ((1, 16), (2, 8)), -0.2, 0.2)), 0.19921875, 4.0).astype(jnp.bfloat16)
    return {"object_field": object_field, "probe": probe, "corners": corners, "counts": counts, "amplitude": amplitude}


def reference(object_field, probe, corners, counts, amplitude):
    win_size = WIN
    inverse_area = 1.0 / (win_size * win_size)
    object_now = object_field
    probe_now = probe
    tile_losses = []
    for iteration in range(ITERS):
        flat_corners = corners[iteration].reshape(-1, 2).astype(jnp.int32)
        alive_mask = (jnp.arange(CAP)[None, None, :] < counts[iteration][:, :, None]).reshape(-1).astype(object_now.dtype)
        measured_all = amplitude[iteration].reshape(-1, win_size, win_size)
        probe_cplx = lax.complex(probe_now[:, 0], probe_now[:, 1])

        def visit_slot(carry, item):
            grad_total, probe_sum = carry
            corner, alive, measured = item
            measured = measured.astype(object_now.dtype)
            anchor_zero = jnp.zeros((), jnp.int32)
            window_pix = lax.dynamic_slice(object_now, (anchor_zero, corner[0], corner[1]), (2, win_size, win_size))
            obj_cplx = lax.complex(window_pix[0], window_pix[1])
            far_field = jnp.fft.fft2(probe_cplx * obj_cplx[None], norm='ortho')
            intensity = lax.optimization_barrier(jnp.sum(far_field.real ** 2 + far_field.imag ** 2, axis=0))
            modulus = jnp.sqrt(intensity + 1.0)
            slot_loss = alive * jnp.sum((modulus - measured) ** 2) * inverse_area
            factor = (1.0 - measured / modulus) * (2.0 * inverse_area) * alive
            back_field = jnp.fft.ifft2(factor[None] * far_field, norm='ortho')
            obj_grad = lax.optimization_barrier(jnp.sum(jnp.conj(probe_cplx) * back_field, axis=0))
            probe_part = jnp.conj(obj_cplx)[None] * back_field
            previous = lax.dynamic_slice(grad_total, (anchor_zero, corner[0], corner[1]), (2, win_size, win_size))
            grad_total = lax.dynamic_update_slice(grad_total, previous + jnp.stack([obj_grad.real, obj_grad.imag]), (anchor_zero, corner[0], corner[1]))
            probe_sum = probe_sum + jnp.stack([probe_part.real, probe_part.imag], axis=1)
            return ((grad_total, probe_sum), slot_loss)
        (object_grad, probe_grad), slot_losses = lax.scan(visit_slot, (jnp.zeros_like(object_now), jnp.zeros_like(probe_now)), (flat_corners, alive_mask, measured_all))
        tile_losses.append(slot_losses.reshape(N_ROW, N_COL, CAP).sum(axis=2))
        step_rate = jnp.sum(slot_losses) / (jnp.sum(object_grad * object_grad) + jnp.sum(probe_grad * probe_grad) + 1e-06)
        object_now = object_now - step_rate * object_grad
        probe_now = probe_now - step_rate * probe_grad
    return (object_now, probe_now, jnp.stack(tile_losses))
```

```python
import math

import jax
import jax.numpy as jnp
import numpy as np
from jax import lax
from jax.experimental import pallas as pl
from jax.experimental.pallas import tpu as pltpu
from jax.sharding import PartitionSpec as P

WIN = 256
HALF = 128
MODES = 3
CAP = 2
AREA = float(WIN * WIN)


def split_bf16(value):
    high = value.astype(jnp.bfloat16)
    low = (value - high.astype(jnp.float32)).astype(jnp.bfloat16)
    return high, low


def transform_tables():
    freq = np.arange(HALF)[:, None]
    pixel = np.arange(HALF)[None, :]
    lefts, rights = [], []
    for odd in (0, 1):
        angle = -2.0 * math.pi * (((2 * freq + odd) * pixel) % WIN) / WIN
        cos, sin = np.cos(angle) / math.sqrt(WIN), np.sin(angle) / math.sqrt(WIN)
        matrix = np.block([[cos, -sin], [sin, cos]])
        for table in (matrix, matrix.T):
            table = table.astype(np.float32)
            high = table.astype(jnp.bfloat16)
            low = (table - high.astype(np.float32)).astype(jnp.bfloat16)
            lefts.append(np.concatenate([high, high, low], axis=1))
            rights.append(np.concatenate([high, high, low], axis=0))
    left = np.stack([lefts[0], lefts[2], lefts[1], lefts[3]])
    right = np.stack([rights[1], rights[3], rights[0], rights[2]])
    order = np.concatenate([np.arange(0, WIN, 2), np.arange(1, WIN, 2)])
    shuffle = np.zeros((WIN, WIN), np.float32)
    shuffle[np.arange(WIN), order] = 1.0
    return left, right, np.stack([shuffle, shuffle.T]).astype(jnp.bfloat16)


def left_apply(table, data):
    high, low = split_bf16(data)
    return jnp.dot(table, jnp.concatenate([high, low, high], axis=0), preferred_element_type=jnp.float32)


def right_apply(data, table):
    high, low = split_bf16(data)
    return jnp.dot(jnp.concatenate([high, low, high], axis=1), table, preferred_element_type=jnp.float32)


def slot_kernel(second, last_slot, *refs):
    refs = list(refs)
    place = refs.pop(0)
    rate_ref = refs.pop(0) if second else None
    patch_ref = refs.pop(0)
    patch_grad = refs.pop(0) if second else None
    probe_ref = refs.pop(0)
    probe_grad = refs.pop(0) if second else None
    amp_ref, left_ref, right_ref, shuffle_ref = refs[:4]
    refs = refs[4:]
    before = refs.pop(0) if last_slot else None
    out_grad, out_probe, out_loss, obj, field, factor = refs
    row, col, alive = place[0], place[1], place[2]

    def probe_plane(index):
        plane = probe_ref[index]
        if second:
            step = jnp.concatenate([probe_grad[2 * index], probe_grad[2 * index + 1]], axis=1)
            plane = plane - rate_ref[0] * step
        return plane

    for part in range(2):
        value = patch_ref[part]
        if second:
            value = value - rate_ref[0] * patch_grad[part]
        value = pltpu.roll(value, (WIN - row) % WIN, 0)
        obj[part] = pltpu.roll(value, (WIN - col) % WIN, 1)

    for mode in range(MODES):
        probe_re, probe_im = probe_plane(2 * mode), probe_plane(2 * mode + 1)
        exit_re = probe_re * obj[0] - probe_im * obj[1]
        exit_im = probe_re * obj[1] + probe_im * obj[0]
        half = []
        for odd in range(2):
            sign = -1.0 if odd else 1.0
            folded = jnp.concatenate(
                [exit_re[:HALF] + sign * exit_re[HALF:], exit_im[:HALF] + sign * exit_im[HALF:]], axis=0
            )
            half.append(left_apply(left_ref[odd], folded))
        mid_re = jnp.concatenate([half[0][:HALF], half[1][:HALF]], axis=0)
        mid_im = jnp.concatenate([half[0][HALF:], half[1][HALF:]], axis=0)
        for odd in range(2):
            sign = -1.0 if odd else 1.0
            folded = jnp.concatenate(
                [mid_re[:, :HALF] + sign * mid_re[:, HALF:], mid_im[:, :HALF] + sign * mid_im[:, HALF:]], axis=1
            )
            field[mode, odd] = right_apply(folded, right_ref[odd])

    amp = jnp.dot(shuffle_ref[0], amp_ref[...], preferred_element_type=jnp.float32).astype(jnp.bfloat16)
    amp = jnp.dot(amp, shuffle_ref[1], preferred_element_type=jnp.float32)
    loss = jnp.zeros((WIN, HALF), jnp.float32)
    for odd in range(2):
        total = jnp.ones((WIN, HALF), jnp.float32)
        for mode in range(MODES):
            real, imag = field[mode, odd, :, :HALF], field[mode, odd, :, HALF:]
            total = total + (real * real + imag * imag)
        inverse = lax.rsqrt(total)
        measured = amp[:, odd * HALF : (odd + 1) * HALF]
        gap = total * inverse - measured
        loss = loss + gap * gap
        factor[odd] = (1.0 - measured * inverse) * (2.0 / AREA * alive.astype(jnp.float32))
    out_loss[...] = jnp.sum(loss.reshape(WIN // 8, 8, HALF), axis=0) * (alive.astype(jnp.float32) / AREA)

    grad_re = jnp.zeros((WIN, WIN), jnp.float32)
    grad_im = jnp.zeros((WIN, WIN), jnp.float32)
    for mode in range(MODES):
        half = []
        for odd in range(2):
            scale = jnp.concatenate([factor[odd], factor[odd]], axis=1)
            half.append(right_apply(field[mode, odd] * scale, right_ref[2 + odd]))
        mid_re = jnp.concatenate(
            [half[0][:, :HALF] + half[1][:, :HALF], half[0][:, :HALF] - half[1][:, :HALF]], axis=1
        )
        mid_im = jnp.concatenate(
            [half[0][:, HALF:] + half[1][:, HALF:], half[0][:, HALF:] - half[1][:, HALF:]], axis=1
        )
        back = []
        for odd in range(2):
            rows = slice(odd * HALF, (odd + 1) * HALF)
            back.append(left_apply(left_ref[2 + odd], jnp.concatenate([mid_re[rows], mid_im[rows]], axis=0)))
        back_re = jnp.concatenate([back[0][:HALF] + back[1][:HALF], back[0][:HALF] - back[1][:HALF]], axis=0)
        back_im = jnp.concatenate([back[0][HALF:] + back[1][HALF:], back[0][HALF:] - back[1][HALF:]], axis=0)
        probe_re, probe_im = probe_plane(2 * mode), probe_plane(2 * mode + 1)
        grad_re = grad_re + (probe_re * back_re + probe_im * back_im)
        grad_im = grad_im + (probe_re * back_im - probe_im * back_re)
        terms = (obj[0] * back_re + obj[1] * back_im, obj[0] * back_im - obj[1] * back_re)
        for part in range(2):
            for side in range(2):
                index = (2 * mode + part) * 2 + side
                value = terms[part][:, side * HALF : (side + 1) * HALF]
                if last_slot:
                    value = value + before[index]
                out_probe[index] = value
    for part, value in enumerate((grad_re, grad_im)):
        out_grad[part] = pltpu.roll(pltpu.roll(value, row, 0), col, 1)


def run_slot(place, rate, patch, patch_grad, probe, probe_grad, amp, tables, before):
    second, last_slot = rate is not None, before is not None
    smem, vmem = pl.BlockSpec(memory_space=pltpu.SMEM), pl.BlockSpec(memory_space=pltpu.VMEM)
    args, specs = [place], [smem]
    if second:
        args.append(rate), specs.append(smem)
    big = [patch] + ([patch_grad] if second else []) + [probe] + ([probe_grad] if second else [])
    big += [amp, *tables] + ([before] if last_slot else [])
    args += big
    specs += [vmem] * len(big)
    return pl.pallas_call(
        lambda *refs: slot_kernel(second, last_slot, *refs),
        out_shape=(
            jax.ShapeDtypeStruct((2, WIN, WIN), jnp.float32),
            jax.ShapeDtypeStruct((4 * MODES, WIN, HALF), jnp.float32),
            jax.ShapeDtypeStruct((8, HALF), jnp.float32),
        ),
        in_specs=specs,
        out_specs=(vmem, vmem, vmem),
        scratch_shapes=[
            pltpu.VMEM((2, WIN, WIN), jnp.float32),
            pltpu.VMEM((MODES, 2, WIN, WIN), jnp.float32),
            pltpu.VMEM((2, WIN, HALF), jnp.float32),
        ],
        compiler_params=pltpu.CompilerParams(vmem_limit_bytes=40 * 1024 * 1024),
        cost_estimate=pl.CostEstimate(flops=5_000_000_000, bytes_accessed=6_000_000, transcendentals=65536),
    )(*args)


def shift(value, axis, steps):
    count = lax.axis_size(axis)
    first, last = max(0, -steps), min(count, count - steps)
    return lax.ppermute(value, axis, [(source, source + steps) for source in range(first, last)])


def row_mask(corner):
    return (lax.broadcasted_iota(jnp.int32, (WIN, WIN), 0) >= corner[0] % WIN)[None]


def col_mask(corner):
    return (lax.broadcasted_iota(jnp.int32, (WIN, WIN), 1) >= corner[1] % WIN)[None]


def block_of(corner):
    return (corner[1] // WIN) % 2


def pick(blocks, corner):
    left = block_of(corner) == 0
    return jnp.where(
        col_mask(corner), jnp.where(left, blocks[0], blocks[1]), jnp.where(left, blocks[1], blocks[2])
    )


def spread(window, corner, block):
    here = jnp.where(block_of(corner) == block, col_mask(corner), False)
    spill = jnp.where(block_of(corner) == block - 1, ~col_mask(corner), False)
    return jnp.where(here | spill, window, 0.0)


def body(object_field, probe, corners, counts, amplitude):
    core_pairs = lax.axis_size("col") // 2
    row_count = lax.axis_size("row")
    core = lax.axis_index("col") % 2
    layers = [[2 * z + c for z in range(core_pairs)] for c in range(2)]
    swap = [(c, c ^ 1) for c in range(2 * core_pairs)]
    tables = [jnp.asarray(table) for table in transform_tables()]
    probe = probe.reshape(2 * MODES, WIN, WIN)
    corners = corners[:, 0, 0]
    corners_above = shift(corners, "row", 1)
    corners_below = shift(corners, "row", -1)
    rim = shift(object_field[:, :, :WIN], "col", -1)
    blocks = [object_field[:, :, :WIN], object_field[:, :, WIN:], rim]

    def place_of(iteration, slot):
        corner = corners[iteration, slot]
        alive = (slot < counts[iteration, 0, 0]).astype(jnp.int32)
        return jnp.stack([corner[0] % WIN, corner[1] % WIN, alive])

    def patch_of(iteration, slot, after=None):
        packed = pick(blocks, corners_above[iteration, slot])
        if after is not None:
            packed, after = lax.optimization_barrier((packed, after))
        below = shift(packed, "row", -1)
        return jnp.where(row_mask(corners[iteration, slot]), pick(blocks, corners[iteration, slot]), below)

    def reduce_scatter(value):
        value = value.reshape(2, core_pairs * row_count, -1, HALF)
        other = lax.ppermute(lax.dynamic_index_in_dim(value, 1 - core, 0, keepdims=False), "col", swap)
        mine = lax.dynamic_index_in_dim(value, core, 0, keepdims=False) + other
        mine = mine.reshape(core_pairs, row_count, -1, HALF)
        mine = lax.all_to_all(mine, "col", 0, 0, axis_index_groups=layers, tiled=True).sum(axis=0)
        return lax.all_to_all(mine, "row", 0, 0, tiled=True).sum(axis=0)

    def all_gather(chunk, scalars):
        depth = chunk.shape[0]
        sent = jnp.concatenate([chunk, scalars], axis=0)
        got = lax.all_to_all(jnp.broadcast_to(sent[None], (row_count, *sent.shape)), "row", 0, 0, tiled=True)
        sent = jnp.concatenate([got[:, :depth].reshape(-1, HALF), got[:, depth:].sum(axis=0)], axis=0)
        got = lax.all_to_all(
            jnp.broadcast_to(sent[None], (core_pairs, *sent.shape)),
            "col", 0, 0, axis_index_groups=layers, tiled=True,
        )
        depth *= row_count
        mine, sums = got[:, :depth].reshape(-1, HALF), got[:, depth:].sum(axis=0)
        other = lax.ppermute(mine, "col", swap)
        sums = sums + lax.ppermute(sums, "col", swap)
        halves = jnp.where(core == 0, jnp.stack([mine, other]), jnp.stack([other, mine]))
        return halves.reshape(4 * MODES, WIN, HALF), sums

    def scalar_rows(loss, square_object, square_probe):
        lane = lax.broadcasted_iota(jnp.int32, (8, HALF), 0)
        return jnp.where(lane == 0, loss, jnp.where(lane == 1, square_object, jnp.where(lane == 2, square_probe, 0.0)))

    def finish(chunk, loss, tile_grad):
        square_object = jnp.sum(tile_grad * tile_grad)
        gathered, sums = all_gather(chunk, scalar_rows(loss, square_object, jnp.sum(chunk * chunk)))
        rate = sums[0, 0] / (sums[1, 0] + sums[2, 0] + 1e-06)
        return gathered, rate

    patches = [patch_of(0, slot) for slot in range(CAP)]
    grads, ups, downs, losses, probe_part = [], [], [], [], None
    for slot in range(CAP):
        grad, probe_part, loss = run_slot(
            place_of(0, slot), None, patches[slot], None, probe, None, amplitude[0, 0, 0, slot], tables, probe_part
        )
        grads.append(grad)
        downs.append(shift(grad, "row", 1))
        ups.append(shift(grad, "row", -1))
        losses.append(loss)
    loss_first = sum(jnp.sum(loss) for loss in losses)
    chunk = reduce_scatter(probe_part)
    next_patches = [patch_of(1, slot, chunk) for slot in range(CAP)]

    def column_block(block):
        top, bottom = 0.0, 0.0
        for slot in range(CAP):
            own = spread(grads[slot], corners[0, slot], block)
            mask = row_mask(corners[0, slot])
            above = spread(downs[slot], corners_above[0, slot], block)
            below = spread(ups[slot], corners_below[0, slot], block)
            top = top + jnp.where(mask, own, 0.0) + jnp.where(row_mask(corners_above[0, slot]), 0.0, above)
            bottom = bottom + jnp.where(mask, 0.0, own) + jnp.where(row_mask(corners_below[0, slot]), below, 0.0)
        return jnp.stack([top, bottom])

    sums = [column_block(block) for block in range(3)]
    from_left = shift(sums[2], "col", 1)
    from_right = shift(sums[0], "col", -1)
    sums = [sums[0] + from_left, sums[1], sums[2] + from_right]
    tile_grad = jnp.concatenate([sums[0][0], sums[1][0]], axis=2)
    patch_grads = [
        jnp.where(
            row_mask(corners[1, slot]),
            pick([s[0] for s in sums], corners[1, slot]),
            pick([s[1] for s in sums], corners[1, slot]),
        )
        for slot in range(CAP)
    ]
    probe_grad, rate = finish(chunk, loss_first, tile_grad)
    object_mid = object_field - rate * tile_grad

    grads, downs, losses, probe_part = [], [], [], None
    for slot in range(CAP):
        grad, probe_part, loss = run_slot(
            place_of(1, slot), rate[None], next_patches[slot], patch_grads[slot], probe, probe_grad,
            amplitude[1, 0, 0, slot], tables, probe_part,
        )
        grads.append(grad)
        downs.append(shift(grad, "row", 1))
        losses.append(loss)
    loss_second = sum(jnp.sum(loss) for loss in losses)
    chunk = reduce_scatter(probe_part)

    def top_block(block):
        top = 0.0
        for slot in range(CAP):
            own = spread(grads[slot], corners[1, slot], block)
            above = spread(downs[slot], corners_above[1, slot], block)
            top = top + jnp.where(row_mask(corners[1, slot]), own, 0.0)
            top = top + jnp.where(row_mask(corners_above[1, slot]), 0.0, above)
        return top

    from_left = shift(top_block(2), "col", 1)
    tile_grad = jnp.concatenate([top_block(0) + from_left, top_block(1)], axis=2)
    probe_step, rate_second = finish(chunk, loss_second, tile_grad)
    object_out = object_mid - rate_second * tile_grad

    def unflatten(value):
        return value.reshape(2 * MODES, 2, WIN, HALF).transpose(0, 2, 1, 3).reshape(2 * MODES, WIN, WIN)

    probe_out = (probe - rate * unflatten(probe_grad)) - rate_second * unflatten(probe_step)
    losses_out = jnp.stack([loss_first, loss_second]).reshape(2, 1, 1)
    return (object_out, probe_out.reshape(MODES, 2, WIN, WIN), losses_out)


def solution(mesh):
    in_specs = (
        P(None, "row", "col"),
        P(),
        P(None, "row", "col", None, None),
        P(None, "row", "col"),
        P(None, "row", "col", None, None, None),
    )
    out_specs = (P(None, "row", "col"), P(), P(None, "row", "col"))
    return jax.shard_map(body, mesh=mesh, in_specs=in_specs, out_specs=out_specs, check_vma=False)
```

```python
import math

import jax
import jax.numpy as jnp
import numpy as np
from jax import lax
from jax.experimental import pallas as pl
from jax.experimental.pallas import tpu as pltpu
from jax.sharding import Mesh
from jax.sharding import PartitionSpec as P

WIN = 256
HALF = 128
MODES = 3
CAP = 2
AREA = float(WIN * WIN)
CHUNK = 24
INFO = 8
SENT = 32
MEGA = 1024 * 1024
F32 = jnp.float32
SMEM = pl.BlockSpec(memory_space=pltpu.SMEM)
VMEM = pl.BlockSpec(memory_space=pltpu.VMEM)
ANY = pl.BlockSpec(memory_space=pl.ANY)


def f32(*shape):
    return jax.ShapeDtypeStruct(shape, F32)


def split_bf16(value):
    high = value.astype(jnp.bfloat16)
    low = (value - high.astype(F32)).astype(jnp.bfloat16)
    return high, low


def transform_tables():
    freq = np.arange(HALF)[:, None]
    pixel = np.arange(HALF)[None, :]
    tables = []
    for odd in (0, 1):
        angle = -2.0 * math.pi * (((2 * freq + odd) * pixel) % WIN) / WIN
        cos, sin = np.cos(angle) / math.sqrt(WIN), np.sin(angle) / math.sqrt(WIN)
        tables.append(np.block([[cos, -sin], [sin, cos]]).astype(np.float32))
    tables = np.stack([tables[0], tables[1], tables[0].T, tables[1].T])
    high = tables.astype(jnp.bfloat16)
    low = (tables - high.astype(np.float32)).astype(jnp.bfloat16)
    order = np.concatenate([np.arange(0, WIN, 2), np.arange(1, WIN, 2)])
    shuffle = np.zeros((WIN, WIN), np.float32)
    shuffle[np.arange(WIN), order] = 1.0
    return np.stack([high, low], axis=1), np.stack([shuffle, shuffle.T]).astype(jnp.bfloat16)


def product(left, right):
    return jnp.dot(left, right, preferred_element_type=F32)


def left_apply(table_ref, index, data):
    high, low = split_bf16(data)
    table = jnp.concatenate([table_ref[index, 0], table_ref[index, 0], table_ref[index, 1]], axis=1)
    return product(table, jnp.concatenate([high, low, high], axis=0))


def right_apply(data, table_ref, index):
    high, low = split_bf16(data)
    table = jnp.concatenate([table_ref[index, 0], table_ref[index, 0], table_ref[index, 1]], axis=0)
    return product(jnp.concatenate([high, low, high], axis=1), table)


def row_place(shape=(WIN, WIN)):
    return lax.broadcasted_iota(jnp.int32, shape, 0)


def col_place(shape=(WIN, WIN)):
    return lax.broadcasted_iota(jnp.int32, shape, 1)


def corner_of(corner_ref, iteration, slot):
    row, col = corner_ref[iteration, slot, 0], corner_ref[iteration, slot, 1]
    return lax.rem(row, WIN), lax.rem(col, WIN), lax.rem(lax.div(col, WIN), 2)


def cut(corner, upper, lower):
    row, col, block = corner
    first = row_place() >= row
    blocks = [jnp.where(first, above, below) for above, below in zip(upper, lower)]
    left = jnp.where(block == 0, blocks[0], blocks[1])
    right = jnp.where(block == 0, blocks[1], blocks[2])
    value = jnp.where(col_place() >= col, left, right)
    value = pltpu.roll(value, lax.rem(WIN - row, WIN), 0)
    return pltpu.roll(value, lax.rem(WIN - col, WIN), 1)


def rate_of(mine, other):
    total = jnp.sum(mine[:, CHUNK:], axis=0) + jnp.sum(other[:, CHUNK:], axis=0)
    return total[0:1] / (total[1:2] + 1e-06)


def gathered_plane(half, index):
    pieces, row, end = [], index * WIN, (index + 1) * WIN
    while row < end:
        chunk, offset = divmod(row, CHUNK)
        size = min(CHUNK - offset, end - row)
        pieces.append(half[chunk, offset : offset + size])
        row += size
    return jnp.concatenate(pieces, axis=0)


def probe_step(mine, other, core):
    planes = []
    for plane in range(2 * MODES):
        sides = []
        for side in range(2):
            half, index = divmod(2 * plane + side, 2 * MODES)
            own, swapped = gathered_plane(mine, index), gathered_plane(other, index)
            sides.append(jnp.where(core == half, own, swapped))
        planes.append(jnp.concatenate(sides, axis=1))
    return planes


def window_kernel(iteration, corner_ref, count_ref, *refs):
    refs = list(refs)
    core = lax.axis_index("core")
    n_big = 9 if iteration == 0 else 8
    sources, refs = refs[:n_big], refs[n_big:]
    out_grad, out_keep, out_send = refs[:3]
    refs = refs[3:]
    if iteration:
        out_mid, out_rate = refs[:2]
        refs = refs[2:]
    out_loss, obj, field, factor, total_probe, grads, sems, out_sems, probe_sems, mid_sem = refs[:10]
    held = refs[10:]
    fetch = [pltpu.make_async_copy(src, dst, sems.at[k]) for k, (src, dst) in enumerate(zip(sources, held))]
    for copy in fetch:
        copy.start()
    if iteration == 0:
        tile, below0, below1, rim, diag, probe_ref, tables, amp_ref, shuffle = held
    else:
        mine, other, patch, patch_grad, probe_ref, tables, amp_ref, shuffle = held
    for copy in fetch[:-3]:
        copy.wait()

    if iteration:
        rate = rate_of(mine, other)
        out_rate[...] = jnp.broadcast_to(rate, (8, HALF))
        wide = jnp.concatenate([rate, rate], axis=1)
        for plane, step in enumerate(probe_step(mine, other, core)):
            probe_ref[plane] = probe_ref[plane] - wide * step
        mid_copy = pltpu.make_async_copy(probe_ref, out_mid, mid_sem.at[0])
        mid_copy.start()

    def deliver(index):
        half, place = divmod(index, 2 * MODES)
        keep = pltpu.make_async_copy(total_probe.at[index], out_keep.at[place], probe_sems.at[index])
        send = pltpu.make_async_copy(total_probe.at[index], out_send.at[place], probe_sems.at[index])
        return half, keep, send

    losses = jnp.zeros((8, HALF), F32)
    for slot in range(CAP):
        corner = corner_of(corner_ref, iteration, slot)
        alive = (slot < count_ref[iteration]).astype(F32)
        for part in range(2):
            if iteration == 0:
                obj[part] = cut(
                    corner,
                    (tile[part, :, :WIN], tile[part, :, WIN:], rim[part]),
                    (below0[part], below1[part], diag[part]),
                )
            else:
                obj[part] = patch[slot, part] - wide * patch_grad[slot, part]

        if slot == 0:
            fetch[-3].wait()
        for mode in range(MODES):
            probe_re, probe_im = probe_ref[2 * mode], probe_ref[2 * mode + 1]
            exit_re = probe_re * obj[0] - probe_im * obj[1]
            exit_im = probe_re * obj[1] + probe_im * obj[0]
            half = []
            for odd in range(2):
                sign = -1.0 if odd else 1.0
                folded = jnp.concatenate(
                    [exit_re[:HALF] + sign * exit_re[HALF:], exit_im[:HALF] + sign * exit_im[HALF:]], axis=0
                )
                half.append(left_apply(tables, odd, folded))
            mid_re = jnp.concatenate([half[0][:HALF], half[1][:HALF]], axis=0)
            mid_im = jnp.concatenate([half[0][HALF:], half[1][HALF:]], axis=0)
            for odd in range(2):
                sign = -1.0 if odd else 1.0
                folded = jnp.concatenate(
                    [mid_re[:, :HALF] + sign * mid_re[:, HALF:], mid_im[:, :HALF] + sign * mid_im[:, HALF:]], axis=1
                )
                field[mode, odd] = right_apply(folded, tables, 2 + odd)

        if slot == 0:
            fetch[-2].wait()
            fetch[-1].wait()
        amp = product(shuffle[0], amp_ref[iteration, slot]).astype(jnp.bfloat16)
        amp = product(amp, shuffle[1])
        loss = jnp.zeros((WIN, HALF), F32)
        for odd in range(2):
            total = jnp.ones((WIN, HALF), F32)
            for mode in range(MODES):
                real, imag = field[mode, odd, :, :HALF], field[mode, odd, :, HALF:]
                total = total + (real * real + imag * imag)
            inverse = lax.rsqrt(total)
            measured = amp[:, odd * HALF : (odd + 1) * HALF]
            gap = total * inverse - measured
            loss = loss + gap * gap
            factor[odd] = (1.0 - measured * inverse) * (2.0 / AREA * alive)
        losses = losses + jnp.sum(loss.reshape(WIN // 8, 8, HALF), axis=0) * (alive / AREA)

        grad_re = jnp.zeros((WIN, WIN), F32)
        grad_im = jnp.zeros((WIN, WIN), F32)
        for mode in range(MODES):
            half = []
            for odd in range(2):
                scale = jnp.concatenate([factor[odd], factor[odd]], axis=1)
                half.append(right_apply(field[mode, odd] * scale, tables, odd))
            mid_re = jnp.concatenate(
                [half[0][:, :HALF] + half[1][:, :HALF], half[0][:, :HALF] - half[1][:, :HALF]], axis=1
            )
            mid_im = jnp.concatenate(
                [half[0][:, HALF:] + half[1][:, HALF:], half[0][:, HALF:] - half[1][:, HALF:]], axis=1
            )
            back = []
            for odd in range(2):
                rows = slice(odd * HALF, (odd + 1) * HALF)
                back.append(left_apply(tables, 2 + odd, jnp.concatenate([mid_re[rows], mid_im[rows]], axis=0)))
            back_re = jnp.concatenate([back[0][:HALF] + back[1][:HALF], back[0][:HALF] - back[1][:HALF]], axis=0)
            back_im = jnp.concatenate([back[0][HALF:] + back[1][HALF:], back[0][HALF:] - back[1][HALF:]], axis=0)
            probe_re, probe_im = probe_ref[2 * mode], probe_ref[2 * mode + 1]
            grad_re = grad_re + (probe_re * back_re + probe_im * back_im)
            grad_im = grad_im + (probe_re * back_im - probe_im * back_re)
            terms = (obj[0] * back_re + obj[1] * back_im, obj[0] * back_im - obj[1] * back_re)
            for part in range(2):
                for side in range(2):
                    index = (2 * mode + part) * 2 + side
                    value = terms[part][:, side * HALF : (side + 1) * HALF]
                    if slot:
                        value = value + total_probe[index]
                    total_probe[index] = value
                    if slot:
                        half, keep, send = deliver(index)
                        pl.when(core == half)(keep.start)
                        pl.when(core != half)(send.start)
        for part, value in enumerate((grad_re, grad_im)):
            grads[slot, part, :WIN] = pltpu.roll(pltpu.roll(value, corner[0], 0), corner[1], 1)
            row = row_place((INFO, WIN))
            info = jnp.where(row == 0, corner[0], jnp.where(row == 1, corner[1], corner[2]))
            grads[slot, part, WIN:] = info.astype(F32)
        pltpu.make_async_copy(grads.at[slot], out_grad.at[slot], out_sems.at[slot]).start()
    out_loss[...] = losses
    for index in range(4 * MODES):
        half, keep, send = deliver(index)
        pl.when(core == half)(keep.wait)
        pl.when(core != half)(send.wait)
    for slot in range(CAP):
        pltpu.make_async_copy(grads.at[slot], out_grad.at[slot], out_sems.at[slot]).wait()
    if iteration:
        mid_copy.wait()


def call(kernel, args, out_shape, n_smem):
    size = sum(math.prod(a.shape) * a.dtype.itemsize for a in (*args, *out_shape))
    return pl.pallas_call(
        kernel,
        out_shape=tuple(out_shape),
        in_specs=[SMEM] * n_smem + [VMEM] * (len(args) - n_smem),
        out_specs=tuple([VMEM] * len(out_shape)),
        compiler_params=pltpu.CompilerParams(vmem_limit_bytes=60 * MEGA),
        cost_estimate=pl.CostEstimate(flops=10_000_000, bytes_accessed=size, transcendentals=0),
    )(*args)


def window_call(iteration, corners, counts, data, amplitude, tables):
    outs = [f32(CAP, 2, WIN + INFO, WIN), f32(2 * MODES, WIN, HALF), f32(2 * MODES, WIN, HALF)]
    out_specs = [ANY] * 3
    if iteration:
        outs += [f32(2 * MODES, WIN, WIN), f32(8, HALF)]
        out_specs += [ANY, VMEM]
    big = [*data, tables[0], amplitude, tables[1]]
    return pl.pallas_call(
        lambda *refs: window_kernel(iteration, *refs),
        out_shape=(*outs, f32(8, HALF)),
        in_specs=[SMEM] * 2 + [ANY] * len(big),
        out_specs=(*out_specs, VMEM),
        scratch_shapes=[
            pltpu.VMEM((2, WIN, WIN), F32),
            pltpu.VMEM((MODES, 2, WIN, WIN), F32),
            pltpu.VMEM((2, WIN, HALF), F32),
            pltpu.VMEM((4 * MODES, WIN, HALF), F32),
            pltpu.VMEM((CAP, 2, WIN + INFO, WIN), F32),
            pltpu.SemaphoreType.DMA((len(big),)),
            pltpu.SemaphoreType.DMA((CAP,)),
            pltpu.SemaphoreType.DMA((4 * MODES,)),
            pltpu.SemaphoreType.DMA((1,)),
            *[pltpu.VMEM(value.shape, value.dtype) for value in big],
        ],
        compiler_params=pltpu.CompilerParams(vmem_limit_bytes=60 * MEGA),
        cost_estimate=pl.CostEstimate(flops=8_000_000_000, bytes_accessed=12_000_000, transcendentals=0),
    )(corners, counts, *big)


def fold_kernel(both, *refs):
    *refs, token, out0, out1, out2 = refs
    outs = (out0, out1, out2)
    rows, cols = row_place(), col_place((1, WIN))
    masks = []
    for windows in refs:
        for slot in range(CAP):
            info = windows[slot, 0, WIN:].astype(jnp.int32)
            masks.append((rows >= info[0:1], jnp.where(cols >= info[1:2], info[2:3], info[2:3] + 1)))
    for part in range(2):
        top, bottom = [0.0] * 3, [0.0] * 3
        for which, windows in enumerate(refs):
            for slot in range(CAP):
                first, target = masks[which * CAP + slot]
                window = windows[slot, part, :WIN]
                upper = jnp.where(first, window, 0.0) if which != 1 else None
                lower = jnp.where(first, 0.0, window) if which != 2 else None
                for index in range(3):
                    here = target == index
                    if which == 0:
                        top[index] += jnp.where(here, upper, 0.0)
                        if both:
                            bottom[index] += jnp.where(here, lower, 0.0)
                    elif which == 1:
                        top[index] += jnp.where(here, lower, 0.0)
                    else:
                        bottom[index] += jnp.where(here, upper, 0.0)
        for index in range(3):
            outs[index][0, part] = top[index]
            if both:
                outs[index][1, part] = bottom[index]
    outs[0][0, 0, :8, :HALF] = outs[0][0, 0, :8, :HALF] + token[...]


def add_kernel(keep, other, out):
    out[...] = keep[...] + other[...]


def sum_kernel(parts, out, out_token):
    out[...] = jnp.sum(parts[...], axis=0)
    out_token[...] = jnp.zeros_like(out_token)


def tile_kernel(block0, block1, from_left, parts, loss, loss_before, out_tile, out_sent, out_loss):
    chunk = jnp.sum(parts[...], axis=0)
    square = sum(chunk[k : k + 8] * chunk[k : k + 8] for k in range(0, CHUNK, 8))
    for part in range(2):
        values = (block0[0, part] + from_left[0, part], block1[0, part])
        for index, value in enumerate(values):
            out_tile[part, :, index * WIN : (index + 1) * WIN] = value
            pieces = jnp.sum((value * value).reshape(WIN // 8, 8, WIN), axis=0)
            square = square + (pieces[:, :HALF] + pieces[:, HALF:])
    loss = jnp.sum(loss[...])
    out_loss[...] = jnp.where(col_place((1, 2)) == 0, jnp.sum(loss_before[...]), loss)
    scalars = jnp.where(row_place((SENT - CHUNK, HALF)) == 0, loss, jnp.sum(square))
    value = jnp.concatenate([chunk, scalars], axis=0)
    for index in range(out_sent.shape[0]):
        out_sent[index] = value


def patch_kernel(corner_ref, tile, below0, below1, rim, diag, block0, block1, block2, left, right, out_obj, out_grad):
    for part in range(2):
        upper = (tile[part, :, :WIN], tile[part, :, WIN:], rim[part])
        lower = (below0[part], below1[part], diag[part])
        grad = [
            (block0[k, part] + left[k, part], block1[k, part], block2[k, part] + right[k, part]) for k in range(2)
        ]
        for slot in range(CAP):
            corner = corner_of(corner_ref, 1, slot)
            out_obj[slot, part] = cut(corner, upper, lower)
            out_grad[slot, part] = cut(corner, grad[0], grad[1])


def final_kernel(tile, grad_first, grad_second, rate_first, probe, mine, other, out_tile, out_probe):
    core = lax.axis_index("core")
    rate = rate_of(mine, other)
    wide = jnp.concatenate([rate, rate], axis=1)
    for plane, step in enumerate(probe_step(mine, other, core)):
        out_probe[plane] = probe[plane] - wide * step
    first = jnp.concatenate([rate_first[0:1]] * 4, axis=1)
    second = jnp.concatenate([rate] * 4, axis=1)
    for part in range(2):
        out_tile[part] = (tile[part] - first * grad_first[part]) - second * grad_second[part]


def shift(value, axis, steps):
    count = math.prod(lax.axis_size(a) for a in axis) if isinstance(axis, tuple) else lax.axis_size(axis)
    first, last = max(0, -steps), min(count, count - steps)
    return lax.ppermute(value, axis, [(source, source + steps) for source in range(first, last)])


COL = ("layer", "core")
CHIPS = ("layer", "row")


def body(object_field, probe, corners, counts, amplitude):
    layers, rows = lax.axis_size("layer"), lax.axis_size("row")
    tables = [jnp.asarray(table) for table in transform_tables()]
    probe = probe.reshape(2 * MODES, WIN, WIN)
    corners, counts = corners[:, 0, 0], counts[:, 0, 0]
    amplitude = amplitude[:, 0, 0]

    first_cols = object_field[:, :, :WIN]
    below0 = shift(first_cols, "row", -1)
    rim = shift(first_cols, COL, -1)
    below1 = shift(object_field[:, :, WIN:], "row", -1)
    diag = shift(below0, COL, -1)
    rims = (below0, below1, rim, diag)

    def swap(value):
        return lax.ppermute(value, "core", [(0, 1), (1, 0)])

    def reduce_chips(keep, send):
        (value,) = call(add_kernel, [keep, swap(send)], [f32(*keep.shape)], 0)
        parts = lax.all_to_all(value.reshape(layers, rows * CHUNK, HALF), "layer", 0, 0, tiled=True)
        return call(sum_kernel, [parts], [f32(rows * CHUNK, HALF), f32(8, HALF)], 0)

    def reduce_rows(part):
        return lax.all_to_all(part.reshape(rows, CHUNK, HALF), "row", 0, 0, tiled=True)

    def finish_tile(sums, from_left, parts, loss, loss_before):
        outs = [f32(2, WIN, 2 * WIN), f32(layers * rows, SENT, HALF), f32(1, 2)]
        args = [sums[0], sums[1], from_left, parts, loss, loss_before]
        tile, sent, losses = call(tile_kernel, args, outs, 0)
        return tile, lax.all_to_all(sent, CHIPS, 0, 0, tiled=True), losses

    def fold(*windows, token):
        both = len(windows) == 3
        strip = f32(1 + both, 2, WIN, WIN)
        return call(lambda *refs: fold_kernel(both, *refs), [*windows, token], [strip] * 3, 0)

    grads, keep, send, loss_first = window_call(
        0, corners, counts, [object_field, *rims, probe], amplitude, tables
    )
    down, up = shift(grads, "row", 1), shift(grads, "row", -1)
    part, token = reduce_chips(keep, send)
    sums = fold(grads, down, up, token=token)
    from_left, from_right = lax.optimization_barrier((shift(sums[2], COL, 1), shift(sums[0], COL, -1)))
    tile_first, mine, _ = finish_tile(sums, from_left, reduce_rows(part), loss_first, loss_first)
    patches = call(
        patch_kernel,
        [corners, object_field, *rims, *sums, from_left, from_right],
        [f32(CAP, 2, WIN, WIN)] * 2,
        1,
    )

    mine, patches = lax.optimization_barrier((mine, patches))

    grads, keep, send, probe_mid, rate_first, loss_second = window_call(
        1, corners, counts, [mine, swap(mine), *patches, probe], amplitude, tables
    )
    down = shift(grads, "row", 1)
    part, token = reduce_chips(keep, send)
    sums = fold(grads, down, token=token)
    from_left = shift(sums[2], COL, 1)
    tile_second, mine, losses = finish_tile(sums, from_left, reduce_rows(part), loss_second, loss_first)
    object_out, probe_out = call(
        final_kernel,
        [object_field, tile_first, tile_second, rate_first, probe_mid, mine, swap(mine)],
        [f32(2, WIN, 2 * WIN), f32(2 * MODES, WIN, WIN)],
        0,
    )
    losses = losses.reshape(1, 1, 2).transpose(2, 0, 1)
    return (object_out, probe_out.reshape(MODES, 2, WIN, WIN), losses)


def solution(mesh):
    rows, cols = mesh.shape["row"], mesh.shape["col"]
    fine = Mesh(mesh.devices.reshape(rows, cols // 2, 2), ("row", "layer", "core"))
    in_specs = (
        P(None, "row", COL),
        P(),
        P(None, "row", COL, None, None),
        P(None, "row", COL),
        P(None, "row", COL, None, None, None),
    )
    out_specs = (P(None, "row", COL), P(), P(None, "row", COL))
    return jax.shard_map(body, mesh=fine, in_specs=in_specs, out_specs=out_specs, check_vma=False)
```

```python
import math

import jax
import jax.numpy as jnp
import numpy as np
from jax import lax
from jax.experimental import pallas as pl
from jax.experimental.pallas import tpu as pltpu
from jax.sharding import Mesh
from jax.sharding import PartitionSpec as P

WIN = 256
HALF = 128
MODES = 3
CAP = 2
AREA = float(WIN * WIN)
CHUNK = 24
INFO = 8
SENT = 32
MEGA = 1024 * 1024
F32 = jnp.float32
SMEM = pl.BlockSpec(memory_space=pltpu.SMEM)
VMEM = pl.BlockSpec(memory_space=pltpu.VMEM)
ANY = pl.BlockSpec(memory_space=pl.ANY)


def f32(*shape):
    return jax.ShapeDtypeStruct(shape, F32)


def split_bf16(value):
    high = value.astype(jnp.bfloat16)
    low = (value - high.astype(F32)).astype(jnp.bfloat16)
    return high, low


def transform_tables():
    freq = np.arange(HALF)[:, None]
    pixel = np.arange(HALF)[None, :]
    tables = []
    for odd in (0, 1):
        angle = -2.0 * math.pi * (((2 * freq + odd) * pixel) % WIN) / WIN
        cos, sin = np.cos(angle) / math.sqrt(WIN), np.sin(angle) / math.sqrt(WIN)
        tables.append(np.block([[cos, -sin], [sin, cos]]).astype(np.float32))
    tables = np.stack([tables[0], tables[1], tables[0].T, tables[1].T])
    high = tables.astype(jnp.bfloat16)
    low = (tables - high.astype(np.float32)).astype(jnp.bfloat16)
    order = np.concatenate([np.arange(0, WIN, 2), np.arange(1, WIN, 2)])
    shuffle = np.zeros((WIN, WIN), np.float32)
    shuffle[np.arange(WIN), order] = 1.0
    return np.stack([high, low], axis=1), np.stack([shuffle, shuffle.T]).astype(jnp.bfloat16)


def product(left, right):
    return jnp.dot(left, right, preferred_element_type=F32)


def left_apply(table_ref, index, data):
    high, low = split_bf16(data)
    table = jnp.concatenate([table_ref[index, 0], table_ref[index, 0], table_ref[index, 1]], axis=1)
    return product(table, jnp.concatenate([high, low, high], axis=0))


def right_apply(lhs, odd, table_ref, index):
    both, high = lhs[odd], lhs[odd, :, :WIN]
    table = jnp.concatenate([table_ref[index, 0], table_ref[index, 0], table_ref[index, 1]], axis=0)
    return product(jnp.concatenate([both, high], axis=1), table)


def row_place(shape=(WIN, WIN)):
    return lax.broadcasted_iota(jnp.int32, shape, 0)


def col_place(shape=(WIN, WIN)):
    return lax.broadcasted_iota(jnp.int32, shape, 1)


def corner_of(corner_ref, iteration, slot):
    row, col = corner_ref[iteration, slot, 0], corner_ref[iteration, slot, 1]
    return lax.rem(row, WIN), lax.rem(col, WIN), lax.rem(lax.div(col, WIN), 2)


def cut(corner, upper, lower):
    row, col, block = corner
    first = row_place() >= row
    blocks = [jnp.where(first, above, below) for above, below in zip(upper, lower)]
    left = jnp.where(block == 0, blocks[0], blocks[1])
    right = jnp.where(block == 0, blocks[1], blocks[2])
    value = jnp.where(col_place() >= col, left, right)
    value = pltpu.roll(value, lax.rem(WIN - row, WIN), 0)
    return pltpu.roll(value, lax.rem(WIN - col, WIN), 1)


def rate_of(mine, other):
    total = jnp.sum(mine[:, CHUNK:], axis=0) + jnp.sum(other[:, CHUNK:], axis=0)
    return total[0:1] / (total[1:2] + 1e-06)


def gathered_plane(half, index):
    pieces, row, end = [], index * WIN, (index + 1) * WIN
    while row < end:
        chunk, offset = divmod(row, CHUNK)
        size = min(CHUNK - offset, end - row)
        pieces.append(half[chunk, offset : offset + size])
        row += size
    return jnp.concatenate(pieces, axis=0)


def probe_step(mine, other, core):
    planes = []
    for plane in range(2 * MODES):
        sides = []
        for side in range(2):
            half, index = divmod(2 * plane + side, 2 * MODES)
            own, swapped = gathered_plane(mine, index), gathered_plane(other, index)
            sides.append(jnp.where(core == half, own, swapped))
        planes.append(jnp.concatenate(sides, axis=1))
    return planes


def window_kernel(iteration, corner_ref, count_ref, *refs):
    refs = list(refs)
    core = lax.axis_index("core")
    n_big = 9 if iteration == 0 else 8
    sources, refs = refs[:n_big], refs[n_big:]
    out_grad, out_keep, out_send = refs[:3]
    refs = refs[3:]
    if iteration:
        out_mid, out_rate = refs[:2]
        refs = refs[2:]
    out_loss, obj, field, lhs, factor, total_probe, grads, sems, out_sems, probe_sems, mid_sem = refs[:11]
    held = refs[11:]
    fetch = [pltpu.make_async_copy(src, dst, sems.at[k]) for k, (src, dst) in enumerate(zip(sources, held))]
    for copy in fetch:
        copy.start()
    if iteration == 0:
        tile, below0, below1, rim, diag, tables, probe_ref, amp_ref, shuffle = held
    else:
        mine, other, probe_ref, patch, patch_grad, tables, amp_ref, shuffle = held
    for copy in fetch[: 5 if iteration == 0 else 3]:
        copy.wait()

    if iteration:
        rate = rate_of(mine, other)
        out_rate[...] = jnp.broadcast_to(rate, (8, HALF))
        wide = jnp.concatenate([rate, rate], axis=1)
        for plane, step in enumerate(probe_step(mine, other, core)):
            probe_ref[plane] = probe_ref[plane] - wide * step
        mid_copy = pltpu.make_async_copy(probe_ref, out_mid, mid_sem.at[0])
        mid_copy.start()

    def deliver(index):
        half, place = divmod(index, 2 * MODES)
        keep = pltpu.make_async_copy(total_probe.at[index], out_keep.at[place], probe_sems.at[index])
        send = pltpu.make_async_copy(total_probe.at[index], out_send.at[place], probe_sems.at[index])
        return half, keep, send

    losses = jnp.zeros((8, HALF), F32)
    for slot in range(CAP):
        corner = corner_of(corner_ref, iteration, slot)
        alive = (slot < count_ref[iteration]).astype(F32)
        if iteration and slot == 0:
            for copy in fetch[3:5]:
                copy.wait()
        for part in range(2):
            if iteration == 0:
                obj[part] = cut(
                    corner,
                    (tile[part, :, :WIN], tile[part, :, WIN:], rim[part]),
                    (below0[part], below1[part], diag[part]),
                )
            else:
                obj[part] = patch[slot, part] - wide * patch_grad[slot, part]

        if slot == 0:
            for copy in fetch[5:-2]:
                copy.wait()
        for mode in range(MODES):
            probe_re, probe_im = probe_ref[2 * mode], probe_ref[2 * mode + 1]
            exit_re = probe_re * obj[0] - probe_im * obj[1]
            exit_im = probe_re * obj[1] + probe_im * obj[0]
            half = []
            for odd in range(2):
                sign = -1.0 if odd else 1.0
                folded = jnp.concatenate(
                    [exit_re[:HALF] + sign * exit_re[HALF:], exit_im[:HALF] + sign * exit_im[HALF:]], axis=0
                )
                half.append(left_apply(tables, odd, folded))
            mid_re = jnp.concatenate([half[0][:HALF], half[1][:HALF]], axis=0)
            mid_im = jnp.concatenate([half[0][HALF:], half[1][HALF:]], axis=0)
            for odd in range(2):
                sign = -1.0 if odd else 1.0
                folded = jnp.concatenate(
                    [mid_re[:, :HALF] + sign * mid_re[:, HALF:], mid_im[:, :HALF] + sign * mid_im[:, HALF:]], axis=1
                )
                high, low = split_bf16(folded)
                rows = slice(mode * WIN, (mode + 1) * WIN)
                lhs[odd, rows, :WIN], lhs[odd, rows, WIN:] = high, low
        for odd in range(2):
            field[odd] = right_apply(lhs, odd, tables, 2 + odd)

        if slot == 0:
            fetch[-2].wait()
            fetch[-1].wait()
        amp = product(shuffle[0], amp_ref[iteration, slot]).astype(jnp.bfloat16)
        amp = product(amp, shuffle[1])
        loss = jnp.zeros((WIN, HALF), F32)
        for odd in range(2):
            total = jnp.ones((WIN, HALF), F32)
            for mode in range(MODES):
                rows = slice(mode * WIN, (mode + 1) * WIN)
                real, imag = field[odd, rows, :HALF], field[odd, rows, HALF:]
                total = total + (real * real + imag * imag)
            inverse = lax.rsqrt(total)
            measured = amp[:, odd * HALF : (odd + 1) * HALF]
            gap = total * inverse - measured
            loss = loss + gap * gap
            factor[odd] = (1.0 - measured * inverse) * (2.0 / AREA * alive)
        losses = losses + jnp.sum(loss.reshape(WIN // 8, 8, HALF), axis=0) * (alive / AREA)

        grad_re = jnp.zeros((WIN, WIN), F32)
        grad_im = jnp.zeros((WIN, WIN), F32)
        for odd in range(2):
            scale = jnp.concatenate([factor[odd], factor[odd]], axis=1)
            for mode in range(MODES):
                rows = slice(mode * WIN, (mode + 1) * WIN)
                high, low = split_bf16(field[odd, rows] * scale)
                lhs[odd, rows, :WIN], lhs[odd, rows, WIN:] = high, low
        for odd in range(2):
            field[odd] = right_apply(lhs, odd, tables, odd)
        for mode in range(MODES):
            half = [field[odd, mode * WIN : (mode + 1) * WIN] for odd in range(2)]
            mid_re = jnp.concatenate(
                [half[0][:, :HALF] + half[1][:, :HALF], half[0][:, :HALF] - half[1][:, :HALF]], axis=1
            )
            mid_im = jnp.concatenate(
                [half[0][:, HALF:] + half[1][:, HALF:], half[0][:, HALF:] - half[1][:, HALF:]], axis=1
            )
            back = []
            for odd in range(2):
                rows = slice(odd * HALF, (odd + 1) * HALF)
                back.append(left_apply(tables, 2 + odd, jnp.concatenate([mid_re[rows], mid_im[rows]], axis=0)))
            back_re = jnp.concatenate([back[0][:HALF] + back[1][:HALF], back[0][:HALF] - back[1][:HALF]], axis=0)
            back_im = jnp.concatenate([back[0][HALF:] + back[1][HALF:], back[0][HALF:] - back[1][HALF:]], axis=0)
            probe_re, probe_im = probe_ref[2 * mode], probe_ref[2 * mode + 1]
            grad_re = grad_re + (probe_re * back_re + probe_im * back_im)
            grad_im = grad_im + (probe_re * back_im - probe_im * back_re)
            terms = (obj[0] * back_re + obj[1] * back_im, obj[0] * back_im - obj[1] * back_re)
            for part in range(2):
                for side in range(2):
                    index = (2 * mode + part) * 2 + side
                    value = terms[part][:, side * HALF : (side + 1) * HALF]
                    if slot:
                        value = value + total_probe[index]
                    total_probe[index] = value
                    if slot:
                        half, keep, send = deliver(index)
                        pl.when(core == half)(keep.start)
                        pl.when(core != half)(send.start)
        for part, value in enumerate((grad_re, grad_im)):
            grads[slot, part, :WIN] = pltpu.roll(pltpu.roll(value, corner[0], 0), corner[1], 1)
            row = row_place((INFO, WIN))
            info = jnp.where(row == 0, corner[0], jnp.where(row == 1, corner[1], corner[2]))
            grads[slot, part, WIN:] = info.astype(F32)
        pltpu.make_async_copy(grads.at[slot], out_grad.at[slot], out_sems.at[slot]).start()
    out_loss[...] = losses
    for index in range(4 * MODES):
        half, keep, send = deliver(index)
        pl.when(core == half)(keep.wait)
        pl.when(core != half)(send.wait)
    for slot in range(CAP):
        pltpu.make_async_copy(grads.at[slot], out_grad.at[slot], out_sems.at[slot]).wait()
    if iteration:
        mid_copy.wait()


def call(kernel, args, out_shape, n_smem):
    size = sum(math.prod(a.shape) * a.dtype.itemsize for a in (*args, *out_shape))
    return pl.pallas_call(
        kernel,
        out_shape=tuple(out_shape),
        in_specs=[SMEM] * n_smem + [VMEM] * (len(args) - n_smem),
        out_specs=tuple([VMEM] * len(out_shape)),
        compiler_params=pltpu.CompilerParams(vmem_limit_bytes=60 * MEGA),
        cost_estimate=pl.CostEstimate(flops=10_000_000, bytes_accessed=size, transcendentals=0),
    )(*args)


def window_call(iteration, corners, counts, data, amplitude, tables):
    outs = [f32(CAP, 2, WIN + INFO, WIN), f32(2 * MODES, WIN, HALF), f32(2 * MODES, WIN, HALF)]
    out_specs = [ANY] * 3
    if iteration:
        outs += [f32(2 * MODES, WIN, WIN), f32(8, HALF)]
        out_specs += [ANY, VMEM]
    big = [*data, amplitude, tables[1]]
    return pl.pallas_call(
        lambda *refs: window_kernel(iteration, *refs),
        out_shape=(*outs, f32(8, HALF)),
        in_specs=[SMEM] * 2 + [ANY] * len(big),
        out_specs=(*out_specs, VMEM),
        scratch_shapes=[
            pltpu.VMEM((2, WIN, WIN), F32),
            pltpu.VMEM((2, MODES * WIN, WIN), F32),
            pltpu.VMEM((2, MODES * WIN, 2 * WIN), jnp.bfloat16),
            pltpu.VMEM((2, WIN, HALF), F32),
            pltpu.VMEM((4 * MODES, WIN, HALF), F32),
            pltpu.VMEM((CAP, 2, WIN + INFO, WIN), F32),
            pltpu.SemaphoreType.DMA((len(big),)),
            pltpu.SemaphoreType.DMA((CAP,)),
            pltpu.SemaphoreType.DMA((4 * MODES,)),
            pltpu.SemaphoreType.DMA((1,)),
            *[pltpu.VMEM(value.shape, value.dtype) for value in big],
        ],
        compiler_params=pltpu.CompilerParams(vmem_limit_bytes=60 * MEGA),
        cost_estimate=pl.CostEstimate(flops=8_000_000_000, bytes_accessed=12_000_000, transcendentals=0),
    )(corners, counts, *big)


def fold_kernel(both, *refs):
    *refs, token, out0, out1, out2 = refs
    outs = (out0, out1, out2)
    rows, cols = row_place(), col_place((1, WIN))
    masks = []
    for windows in refs:
        for slot in range(CAP):
            info = windows[slot, 0, WIN:].astype(jnp.int32)
            masks.append((rows >= info[0:1], jnp.where(cols >= info[1:2], info[2:3], info[2:3] + 1)))
    for part in range(2):
        top, bottom = [0.0] * 3, [0.0] * 3
        for which, windows in enumerate(refs):
            for slot in range(CAP):
                first, target = masks[which * CAP + slot]
                window = windows[slot, part, :WIN]
                upper = jnp.where(first, window, 0.0) if which != 1 else None
                lower = jnp.where(first, 0.0, window) if which != 2 else None
                for index in range(3):
                    here = target == index
                    if which == 0:
                        top[index] += jnp.where(here, upper, 0.0)
                        if both:
                            bottom[index] += jnp.where(here, lower, 0.0)
                    elif which == 1:
                        top[index] += jnp.where(here, lower, 0.0)
                    else:
                        bottom[index] += jnp.where(here, upper, 0.0)
        for index in range(3):
            outs[index][0, part] = top[index]
            if both:
                outs[index][1, part] = bottom[index]
    outs[0][0, 0, :8, :HALF] = outs[0][0, 0, :8, :HALF] + token[...]


def add_kernel(keep, other, out):
    out[...] = keep[...] + other[...]


def sum_kernel(parts, out, out_token):
    out[...] = jnp.sum(parts[...], axis=0)
    out_token[...] = jnp.zeros_like(out_token)


def tile_kernel(block0, block1, from_left, parts, loss, loss_before, out_tile, out_sent, out_loss):
    chunk = jnp.sum(parts[...], axis=0)
    square = sum(chunk[k : k + 8] * chunk[k : k + 8] for k in range(0, CHUNK, 8))
    for part in range(2):
        values = (block0[0, part] + from_left[0, part], block1[0, part])
        for index, value in enumerate(values):
            out_tile[part, :, index * WIN : (index + 1) * WIN] = value
            pieces = jnp.sum((value * value).reshape(WIN // 8, 8, WIN), axis=0)
            square = square + (pieces[:, :HALF] + pieces[:, HALF:])
    loss = jnp.sum(loss[...])
    out_loss[...] = jnp.where(col_place((1, 2)) == 0, jnp.sum(loss_before[...]), loss)
    scalars = jnp.where(row_place((SENT - CHUNK, HALF)) == 0, loss, jnp.sum(square))
    value = jnp.concatenate([chunk, scalars], axis=0)
    for index in range(out_sent.shape[0]):
        out_sent[index] = value


def patch_kernel(corner_ref, tile, below0, below1, rim, diag, block0, block1, block2, left, right, out_obj, out_grad):
    for part in range(2):
        upper = (tile[part, :, :WIN], tile[part, :, WIN:], rim[part])
        lower = (below0[part], below1[part], diag[part])
        grad = [
            (block0[k, part] + left[k, part], block1[k, part], block2[k, part] + right[k, part]) for k in range(2)
        ]
        for slot in range(CAP):
            corner = corner_of(corner_ref, 1, slot)
            out_obj[slot, part] = cut(corner, upper, lower)
            out_grad[slot, part] = cut(corner, grad[0], grad[1])


def final_kernel(rate_first, *refs):
    sources, (out_tile, out_probe) = refs[:6], refs[6:8]
    held, (new_tile, new_probe), sems, tile_sems, probe_sems = refs[8:14], refs[14:16], *refs[16:]
    fetch = [pltpu.make_async_copy(src, dst, sems.at[k]) for k, (src, dst) in enumerate(zip(sources, held))]
    for copy in fetch:
        copy.start()
    mine, other, probe, tile, grad_first, grad_second = held
    core = lax.axis_index("core")
    for copy in fetch[:3]:
        copy.wait()
    rate = rate_of(mine, other)
    wide = jnp.concatenate([rate, rate], axis=1)
    back = []
    for plane, step in enumerate(probe_step(mine, other, core)):
        new_probe[plane] = probe[plane] - wide * step
        back.append(pltpu.make_async_copy(new_probe.at[plane], out_probe.at[plane], probe_sems.at[plane]))
        back[-1].start()
    for copy in fetch[3:]:
        copy.wait()
    first = jnp.concatenate([rate_first[0:1]] * 4, axis=1)
    second = jnp.concatenate([rate] * 4, axis=1)
    for part in range(2):
        new_tile[part] = (tile[part] - first * grad_first[part]) - second * grad_second[part]
        back.append(pltpu.make_async_copy(new_tile.at[part], out_tile.at[part], tile_sems.at[part]))
        back[-1].start()
    for copy in back:
        copy.wait()


def final_call(rate_first, data):
    outs = (f32(2, WIN, 2 * WIN), f32(2 * MODES, WIN, WIN))
    return pl.pallas_call(
        final_kernel,
        out_shape=outs,
        in_specs=[VMEM] + [ANY] * len(data),
        out_specs=(ANY, ANY),
        scratch_shapes=[
            *[pltpu.VMEM(value.shape, value.dtype) for value in (*data, *outs)],
            pltpu.SemaphoreType.DMA((len(data),)),
            pltpu.SemaphoreType.DMA((2,)),
            pltpu.SemaphoreType.DMA((2 * MODES,)),
        ],
        compiler_params=pltpu.CompilerParams(vmem_limit_bytes=60 * MEGA),
        cost_estimate=pl.CostEstimate(flops=10_000_000, bytes_accessed=9_000_000, transcendentals=0),
    )(rate_first, *data)


def shift(value, axis, steps):
    count = math.prod(lax.axis_size(a) for a in axis) if isinstance(axis, tuple) else lax.axis_size(axis)
    first, last = max(0, -steps), min(count, count - steps)
    return lax.ppermute(value, axis, [(source, source + steps) for source in range(first, last)])


COL = ("layer", "core")
CHIPS = ("layer", "row")


def body(object_field, probe, corners, counts, amplitude):
    layers, rows = lax.axis_size("layer"), lax.axis_size("row")
    tables = [jnp.asarray(table) for table in transform_tables()]
    probe = probe.reshape(2 * MODES, WIN, WIN)
    corners, counts = corners[:, 0, 0], counts[:, 0, 0]
    amplitude = amplitude[:, 0, 0]

    first_cols = object_field[:, :, :WIN]
    below0 = shift(first_cols, "row", -1)
    rim = shift(first_cols, COL, -1)
    below1 = shift(object_field[:, :, WIN:], "row", -1)
    diag = shift(below0, COL, -1)
    rims = (below0, below1, rim, diag)

    def swap(value):
        return lax.ppermute(value, "core", [(0, 1), (1, 0)])

    def reduce_chips(keep, send):
        (value,) = call(add_kernel, [keep, swap(send)], [f32(*keep.shape)], 0)
        parts = lax.all_to_all(value.reshape(layers, rows * CHUNK, HALF), "layer", 0, 0, tiled=True)
        return call(sum_kernel, [parts], [f32(rows * CHUNK, HALF), f32(8, HALF)], 0)

    def reduce_rows(part):
        return lax.all_to_all(part.reshape(rows, CHUNK, HALF), "row", 0, 0, tiled=True)

    def finish_tile(sums, from_left, chunk, loss, loss_before):
        outs = [f32(2, WIN, 2 * WIN), f32(layers * rows, SENT, HALF), f32(1, 2)]
        args = [sums[0], sums[1], from_left, chunk, loss, loss_before]
        tile, sent, losses = call(tile_kernel, args, outs, 0)
        return tile, lax.all_to_all(sent, CHIPS, 0, 0, tiled=True), losses

    def fold(*windows, token):
        both = len(windows) == 3
        strip = f32(1 + both, 2, WIN, WIN)
        return call(lambda *refs: fold_kernel(both, *refs), [*windows, token], [strip] * 3, 0)

    grads, keep, send, loss_first = window_call(
        0, corners, counts, [object_field, *rims, tables[0], probe], amplitude, tables
    )
    down, up = shift(grads, "row", 1), shift(grads, "row", -1)
    part, token = reduce_chips(keep, send)
    sums = fold(grads, down, up, token=token)
    chunk, sums = lax.optimization_barrier((reduce_rows(part), sums))
    from_left, from_right = shift(sums[2], COL, 1), shift(sums[0], COL, -1)
    tile_first, mine, _ = finish_tile(sums, from_left, chunk, loss_first, loss_first)
    patches = call(
        patch_kernel,
        [corners, object_field, *rims, *sums, from_left, from_right],
        [f32(CAP, 2, WIN, WIN)] * 2,
        1,
    )

    mine, patches = lax.optimization_barrier((mine, patches))

    grads, keep, send, probe_mid, rate_first, loss_second = window_call(
        1, corners, counts, [mine, swap(mine), probe, *patches, tables[0]], amplitude, tables
    )
    down = shift(grads, "row", 1)
    part, token = reduce_chips(keep, send)
    sums = fold(grads, down, token=token)
    chunk, sums = lax.optimization_barrier((reduce_rows(part), sums))
    from_left = shift(sums[2], COL, 1)
    tile_second, mine, losses = finish_tile(sums, from_left, chunk, loss_second, loss_first)
    object_out, probe_out = final_call(
        rate_first, [mine, swap(mine), probe_mid, object_field, tile_first, tile_second]
    )
    losses = losses.reshape(1, 1, 2).transpose(2, 0, 1)
    return (object_out, probe_out.reshape(MODES, 2, WIN, WIN), losses)


def solution(mesh):
    rows, cols = mesh.shape["row"], mesh.shape["col"]
    fine = Mesh(mesh.devices.reshape(rows, cols // 2, 2), ("row", "layer", "core"))
    in_specs = (
        P(None, "row", COL),
        P(),
        P(None, "row", COL, None, None),
        P(None, "row", COL),
        P(None, "row", COL, None, None, None),
    )
    out_specs = (P(None, "row", COL), P(), P(None, "row", COL))
    return jax.shard_map(body, mesh=fine, in_specs=in_specs, out_specs=out_specs, check_vma=False)
```

```python
import math

import jax
import jax.numpy as jnp
import numpy as np
from jax import lax
from jax.experimental import pallas as pl
from jax.experimental.pallas import tpu as pltpu
from jax.sharding import Mesh
from jax.sharding import PartitionSpec as P

WIN = 256
HALF = 128
MODES = 3
CAP = 2
AREA = float(WIN * WIN)
CHUNK = 24
INFO = 8
SENT = 32
MEGA = 1024 * 1024
F32 = jnp.float32
SMEM = pl.BlockSpec(memory_space=pltpu.SMEM)
VMEM = pl.BlockSpec(memory_space=pltpu.VMEM)
ANY = pl.BlockSpec(memory_space=pl.ANY)


def f32(*shape):
    return jax.ShapeDtypeStruct(shape, F32)


def split_bf16(value):
    high = value.astype(jnp.bfloat16)
    low = (value - high.astype(F32)).astype(jnp.bfloat16)
    return high, low


def transform_tables():
    freq = np.arange(HALF)[:, None]
    pixel = np.arange(HALF)[None, :]
    tables = []
    for odd in (0, 1):
        angle = -2.0 * math.pi * (((2 * freq + odd) * pixel) % WIN) / WIN
        cos, sin = np.cos(angle) / math.sqrt(WIN), np.sin(angle) / math.sqrt(WIN)
        tables.append(np.block([[cos, -sin], [sin, cos]]).astype(np.float32))
    tables = np.stack([tables[0], tables[1], tables[0].T, tables[1].T])
    high = tables.astype(jnp.bfloat16)
    low = (tables - high.astype(np.float32)).astype(jnp.bfloat16)
    order = np.concatenate([np.arange(0, WIN, 2), np.arange(1, WIN, 2)])
    shuffle = np.zeros((WIN, WIN), np.float32)
    shuffle[np.arange(WIN), order] = 1.0
    return np.stack([high, low], axis=1), np.stack([shuffle, shuffle.T]).astype(jnp.bfloat16)


def product(left, right):
    return jnp.dot(left, right, preferred_element_type=F32)


def left_apply(table_ref, index, data):
    high, low = split_bf16(data)
    table = jnp.concatenate([table_ref[index, 0], table_ref[index, 0], table_ref[index, 1]], axis=1)
    return product(table, jnp.concatenate([high, low, high], axis=0))


def right_apply(lhs, odd, table_ref, index):
    both, high = lhs[odd], lhs[odd, :, :WIN]
    table = jnp.concatenate([table_ref[index, 0], table_ref[index, 0], table_ref[index, 1]], axis=0)
    return product(jnp.concatenate([both, high], axis=1), table)


def row_place(shape=(WIN, WIN)):
    return lax.broadcasted_iota(jnp.int32, shape, 0)


def col_place(shape=(WIN, WIN)):
    return lax.broadcasted_iota(jnp.int32, shape, 1)


def corner_of(corner_ref, iteration, slot):
    row, col = corner_ref[iteration, slot, 0], corner_ref[iteration, slot, 1]
    return lax.rem(row, WIN), lax.rem(col, WIN), lax.rem(lax.div(col, WIN), 2)


def cut(corner, upper, lower):
    row, col, block = corner
    first = row_place() >= row
    blocks = [jnp.where(first, above, below) for above, below in zip(upper, lower)]
    left = jnp.where(block == 0, blocks[0], blocks[1])
    right = jnp.where(block == 0, blocks[1], blocks[2])
    value = jnp.where(col_place() >= col, left, right)
    value = pltpu.roll(value, lax.rem(WIN - row, WIN), 0)
    return pltpu.roll(value, lax.rem(WIN - col, WIN), 1)


def rate_of(mine, other):
    total = jnp.sum(mine[:, CHUNK:], axis=0) + jnp.sum(other[:, CHUNK:], axis=0)
    return total[0:1] / (total[1:2] + 1e-06)


def gathered_plane(half, index):
    pieces, row, end = [], index * WIN, (index + 1) * WIN
    while row < end:
        chunk, offset = divmod(row, CHUNK)
        size = min(CHUNK - offset, end - row)
        pieces.append(half[chunk, offset : offset + size])
        row += size
    return jnp.concatenate(pieces, axis=0)


def probe_step(mine, other, core):
    planes = []
    for plane in range(2 * MODES):
        sides = []
        for side in range(2):
            half, index = divmod(2 * plane + side, 2 * MODES)
            own, swapped = gathered_plane(mine, index), gathered_plane(other, index)
            sides.append(jnp.where(core == half, own, swapped))
        planes.append(jnp.concatenate(sides, axis=1))
    return planes


def window_kernel(iteration, corner_ref, count_ref, *refs):
    refs = list(refs)
    core = lax.axis_index("core")
    n_big = 9 if iteration == 0 else 8
    sources, refs = refs[:n_big], refs[n_big:]
    out_grad, out_keep, out_send = refs[:3]
    refs = refs[3:]
    if iteration:
        out_mid, out_rate = refs[:2]
        refs = refs[2:]
    out_loss, obj, field, lhs, factor, total_probe, grads, sems, out_sems, probe_sems, mid_sem = refs[:11]
    held = refs[11:]
    fetch = [pltpu.make_async_copy(src, dst, sems.at[k]) for k, (src, dst) in enumerate(zip(sources, held))]
    for copy in fetch:
        copy.start()
    if iteration == 0:
        tile, below0, below1, rim, diag, tables, probe_ref, amp_ref, shuffle = held
    else:
        mine, other, probe_ref, patch, patch_grad, tables, amp_ref, shuffle = held
    for copy in fetch[: 5 if iteration == 0 else 3]:
        copy.wait()

    if iteration:
        rate = rate_of(mine, other)
        out_rate[...] = jnp.broadcast_to(rate, (8, HALF))
        wide = jnp.concatenate([rate, rate], axis=1)
        for plane, step in enumerate(probe_step(mine, other, core)):
            probe_ref[plane] = probe_ref[plane] - wide * step
        mid_copy = pltpu.make_async_copy(probe_ref, out_mid, mid_sem.at[0])
        mid_copy.start()

    def deliver(index):
        half, place = divmod(index, 2 * MODES)
        keep = pltpu.make_async_copy(total_probe.at[index], out_keep.at[place], probe_sems.at[index])
        send = pltpu.make_async_copy(total_probe.at[index], out_send.at[place], probe_sems.at[index])
        return half, keep, send

    losses = jnp.zeros((8, HALF), F32)
    for slot in range(CAP):
        corner = corner_of(corner_ref, iteration, slot)
        alive = (slot < count_ref[iteration]).astype(F32)
        if iteration and slot == 0:
            for copy in fetch[3:5]:
                copy.wait()
        for part in range(2):
            if iteration == 0:
                obj[part] = cut(
                    corner,
                    (tile[part, :, :WIN], tile[part, :, WIN:], rim[part]),
                    (below0[part], below1[part], diag[part]),
                )
            else:
                obj[part] = patch[slot, part] - wide * patch_grad[slot, part]

        if slot == 0:
            for copy in fetch[5:-2]:
                copy.wait()
        for mode in range(MODES):
            probe_re, probe_im = probe_ref[2 * mode], probe_ref[2 * mode + 1]
            exit_re = probe_re * obj[0] - probe_im * obj[1]
            exit_im = probe_re * obj[1] + probe_im * obj[0]
            half = []
            for odd in range(2):
                sign = -1.0 if odd else 1.0
                folded = jnp.concatenate(
                    [exit_re[:HALF] + sign * exit_re[HALF:], exit_im[:HALF] + sign * exit_im[HALF:]], axis=0
                )
                half.append(left_apply(tables, odd, folded))
            mid_re = jnp.concatenate([half[0][:HALF], half[1][:HALF]], axis=0)
            mid_im = jnp.concatenate([half[0][HALF:], half[1][HALF:]], axis=0)
            for odd in range(2):
                sign = -1.0 if odd else 1.0
                folded = jnp.concatenate(
                    [mid_re[:, :HALF] + sign * mid_re[:, HALF:], mid_im[:, :HALF] + sign * mid_im[:, HALF:]], axis=1
                )
                high, low = split_bf16(folded)
                rows = slice(mode * WIN, (mode + 1) * WIN)
                lhs[odd, rows, :WIN], lhs[odd, rows, WIN:] = high, low
        for odd in range(2):
            field[odd] = right_apply(lhs, odd, tables, 2 + odd)

        if slot == 0:
            fetch[-2].wait()
            fetch[-1].wait()
        amp = product(shuffle[0], amp_ref[iteration, slot]).astype(jnp.bfloat16)
        amp = product(amp, shuffle[1])
        loss = jnp.zeros((WIN, HALF), F32)
        for odd in range(2):
            total = jnp.ones((WIN, HALF), F32)
            for mode in range(MODES):
                rows = slice(mode * WIN, (mode + 1) * WIN)
                real, imag = field[odd, rows, :HALF], field[odd, rows, HALF:]
                total = total + (real * real + imag * imag)
            inverse = lax.rsqrt(total)
            measured = amp[:, odd * HALF : (odd + 1) * HALF]
            gap = total * inverse - measured
            loss = loss + gap * gap
            factor[odd] = (1.0 - measured * inverse) * (2.0 / AREA * alive)
        losses = losses + jnp.sum(loss.reshape(WIN // 8, 8, HALF), axis=0) * (alive / AREA)

        grad_re = jnp.zeros((WIN, WIN), F32)
        grad_im = jnp.zeros((WIN, WIN), F32)
        for odd in range(2):
            scale = jnp.concatenate([factor[odd], factor[odd]], axis=1)
            for mode in range(MODES):
                rows = slice(mode * WIN, (mode + 1) * WIN)
                high, low = split_bf16(field[odd, rows] * scale)
                lhs[odd, rows, :WIN], lhs[odd, rows, WIN:] = high, low
        for odd in range(2):
            field[odd] = right_apply(lhs, odd, tables, odd)
        for mode in range(MODES):
            half = [field[odd, mode * WIN : (mode + 1) * WIN] for odd in range(2)]
            mid_re = jnp.concatenate(
                [half[0][:, :HALF] + half[1][:, :HALF], half[0][:, :HALF] - half[1][:, :HALF]], axis=1
            )
            mid_im = jnp.concatenate(
                [half[0][:, HALF:] + half[1][:, HALF:], half[0][:, HALF:] - half[1][:, HALF:]], axis=1
            )
            back = []
            for odd in range(2):
                rows = slice(odd * HALF, (odd + 1) * HALF)
                back.append(left_apply(tables, 2 + odd, jnp.concatenate([mid_re[rows], mid_im[rows]], axis=0)))
            back_re = jnp.concatenate([back[0][:HALF] + back[1][:HALF], back[0][:HALF] - back[1][:HALF]], axis=0)
            back_im = jnp.concatenate([back[0][HALF:] + back[1][HALF:], back[0][HALF:] - back[1][HALF:]], axis=0)
            probe_re, probe_im = probe_ref[2 * mode], probe_ref[2 * mode + 1]
            grad_re = grad_re + (probe_re * back_re + probe_im * back_im)
            grad_im = grad_im + (probe_re * back_im - probe_im * back_re)
            terms = (obj[0] * back_re + obj[1] * back_im, obj[0] * back_im - obj[1] * back_re)
            for part in range(2):
                for side in range(2):
                    index = (2 * mode + part) * 2 + side
                    value = terms[part][:, side * HALF : (side + 1) * HALF]
                    if slot:
                        value = value + total_probe[index]
                    total_probe[index] = value
                    if slot:
                        half, keep, send = deliver(index)
                        pl.when(core == half)(keep.start)
                        pl.when(core != half)(send.start)
        for part, value in enumerate((grad_re, grad_im)):
            grads[slot, part, :WIN] = pltpu.roll(pltpu.roll(value, corner[0], 0), corner[1], 1)
            row = row_place((INFO, WIN))
            info = jnp.where(row == 0, corner[0], jnp.where(row == 1, corner[1], corner[2]))
            grads[slot, part, WIN:] = info.astype(F32)
        pltpu.make_async_copy(grads.at[slot], out_grad.at[slot], out_sems.at[slot]).start()
    out_loss[...] = losses
    for index in range(4 * MODES):
        half, keep, send = deliver(index)
        pl.when(core == half)(keep.wait)
        pl.when(core != half)(send.wait)
    for slot in range(CAP):
        pltpu.make_async_copy(grads.at[slot], out_grad.at[slot], out_sems.at[slot]).wait()
    if iteration:
        mid_copy.wait()


def call(kernel, args, out_shape, n_smem, limit=60):
    size = sum(math.prod(a.shape) * a.dtype.itemsize for a in (*args, *out_shape))
    return pl.pallas_call(
        kernel,
        out_shape=tuple(out_shape),
        in_specs=[SMEM] * n_smem + [VMEM] * (len(args) - n_smem),
        out_specs=tuple([VMEM] * len(out_shape)),
        compiler_params=pltpu.CompilerParams(vmem_limit_bytes=limit * MEGA),
        cost_estimate=pl.CostEstimate(flops=10_000_000, bytes_accessed=size, transcendentals=0),
    )(*args)


def window_call(iteration, corners, counts, data, amplitude, tables):
    outs = [f32(CAP, 2, WIN + INFO, WIN), f32(2 * MODES, WIN, HALF), f32(2 * MODES, WIN, HALF)]
    out_specs = [ANY] * 3
    if iteration:
        outs += [f32(2 * MODES, WIN, WIN), f32(8, HALF)]
        out_specs += [ANY, VMEM]
    big = [*data, amplitude, tables[1]]
    return pl.pallas_call(
        lambda *refs: window_kernel(iteration, *refs),
        out_shape=(*outs, f32(8, HALF)),
        in_specs=[SMEM] * 2 + [ANY] * len(big),
        out_specs=(*out_specs, VMEM),
        scratch_shapes=[
            pltpu.VMEM((2, WIN, WIN), F32),
            pltpu.VMEM((2, MODES * WIN, WIN), F32),
            pltpu.VMEM((2, MODES * WIN, 2 * WIN), jnp.bfloat16),
            pltpu.VMEM((2, WIN, HALF), F32),
            pltpu.VMEM((4 * MODES, WIN, HALF), F32),
            pltpu.VMEM((CAP, 2, WIN + INFO, WIN), F32),
            pltpu.SemaphoreType.DMA((len(big),)),
            pltpu.SemaphoreType.DMA((CAP,)),
            pltpu.SemaphoreType.DMA((4 * MODES,)),
            pltpu.SemaphoreType.DMA((1,)),
            *[pltpu.VMEM(value.shape, value.dtype) for value in big],
        ],
        compiler_params=pltpu.CompilerParams(vmem_limit_bytes=(60 if iteration else 48) * MEGA),
        cost_estimate=pl.CostEstimate(flops=8_000_000_000, bytes_accessed=12_000_000, transcendentals=0),
    )(corners, counts, *big)


def fold_kernel(both, *refs):
    *refs, token, out0, out1, out2 = refs
    outs = (out0, out1, out2)
    rows, cols = row_place(), col_place((1, WIN))
    masks = []
    for windows in refs:
        for slot in range(CAP):
            info = windows[slot, 0, WIN:].astype(jnp.int32)
            masks.append((rows >= info[0:1], jnp.where(cols >= info[1:2], info[2:3], info[2:3] + 1)))
    for part in range(2):
        top, bottom = [0.0] * 3, [0.0] * 3
        for which, windows in enumerate(refs):
            for slot in range(CAP):
                first, target = masks[which * CAP + slot]
                window = windows[slot, part, :WIN]
                upper = jnp.where(first, window, 0.0) if which != 1 else None
                lower = jnp.where(first, 0.0, window) if which != 2 else None
                for index in range(3):
                    here = target == index
                    if which == 0:
                        top[index] += jnp.where(here, upper, 0.0)
                        if both:
                            bottom[index] += jnp.where(here, lower, 0.0)
                    elif which == 1:
                        top[index] += jnp.where(here, lower, 0.0)
                    else:
                        bottom[index] += jnp.where(here, upper, 0.0)
        for index in range(3):
            outs[index][0, part] = top[index]
            if both:
                outs[index][1, part] = bottom[index]
    outs[0][0, 0, :8, :HALF] = outs[0][0, 0, :8, :HALF] + token[...]


def add_kernel(keep, other, out):
    out[...] = keep[...] + other[...]


def sum_kernel(parts, out, out_token):
    out[...] = jnp.sum(parts[...], axis=0)
    out_token[...] = jnp.zeros_like(out_token)


def tile_kernel(block0, block1, from_left, parts, loss, loss_before, out_tile, out_sent, out_loss):
    chunk = jnp.sum(parts[...], axis=0)
    square = sum(chunk[k : k + 8] * chunk[k : k + 8] for k in range(0, CHUNK, 8))
    for part in range(2):
        values = (block0[0, part] + from_left[0, part], block1[0, part])
        for index, value in enumerate(values):
            out_tile[part, :, index * WIN : (index + 1) * WIN] = value
            pieces = jnp.sum((value * value).reshape(WIN // 8, 8, WIN), axis=0)
            square = square + (pieces[:, :HALF] + pieces[:, HALF:])
    loss = jnp.sum(loss[...])
    out_loss[...] = jnp.where(col_place((1, 2)) == 0, jnp.sum(loss_before[...]), loss)
    scalars = jnp.where(row_place((SENT - CHUNK, HALF)) == 0, loss, jnp.sum(square))
    value = jnp.concatenate([chunk, scalars], axis=0)
    for index in range(out_sent.shape[0]):
        out_sent[index] = value


def patch_kernel(corner_ref, tile, below0, below1, rim, diag, block0, block1, block2, left, right, out_obj, out_grad):
    for part in range(2):
        upper = (tile[part, :, :WIN], tile[part, :, WIN:], rim[part])
        lower = (below0[part], below1[part], diag[part])
        grad = [
            (block0[k, part] + left[k, part], block1[k, part], block2[k, part] + right[k, part]) for k in range(2)
        ]
        for slot in range(CAP):
            corner = corner_of(corner_ref, 1, slot)
            out_obj[slot, part] = cut(corner, upper, lower)
            out_grad[slot, part] = cut(corner, grad[0], grad[1])


def final_kernel(rate_first, *refs):
    sources, (out_tile, out_probe) = refs[:6], refs[6:8]
    held, (new_tile, new_probe), sems, tile_sems, probe_sems = refs[8:14], refs[14:16], *refs[16:]
    fetch = [pltpu.make_async_copy(src, dst, sems.at[k]) for k, (src, dst) in enumerate(zip(sources, held))]
    for copy in fetch:
        copy.start()
    mine, other, probe, tile, grad_first, grad_second = held
    core = lax.axis_index("core")
    for copy in fetch[:3]:
        copy.wait()
    rate = rate_of(mine, other)
    wide = jnp.concatenate([rate, rate], axis=1)
    back = []
    for plane, step in enumerate(probe_step(mine, other, core)):
        new_probe[plane] = probe[plane] - wide * step
        back.append(pltpu.make_async_copy(new_probe.at[plane], out_probe.at[plane], probe_sems.at[plane]))
        back[-1].start()
    for copy in fetch[3:]:
        copy.wait()
    first = jnp.concatenate([rate_first[0:1]] * 4, axis=1)
    second = jnp.concatenate([rate] * 4, axis=1)
    for part in range(2):
        new_tile[part] = (tile[part] - first * grad_first[part]) - second * grad_second[part]
        back.append(pltpu.make_async_copy(new_tile.at[part], out_tile.at[part], tile_sems.at[part]))
        back[-1].start()
    for copy in back:
        copy.wait()


def final_call(rate_first, data):
    outs = (f32(2, WIN, 2 * WIN), f32(2 * MODES, WIN, WIN))
    return pl.pallas_call(
        final_kernel,
        out_shape=outs,
        in_specs=[VMEM] + [ANY] * len(data),
        out_specs=(ANY, ANY),
        scratch_shapes=[
            *[pltpu.VMEM(value.shape, value.dtype) for value in (*data, *outs)],
            pltpu.SemaphoreType.DMA((len(data),)),
            pltpu.SemaphoreType.DMA((2,)),
            pltpu.SemaphoreType.DMA((2 * MODES,)),
        ],
        compiler_params=pltpu.CompilerParams(vmem_limit_bytes=48 * MEGA),
        cost_estimate=pl.CostEstimate(flops=10_000_000, bytes_accessed=9_000_000, transcendentals=0),
    )(rate_first, *data)


def shift(value, axis, steps):
    count = math.prod(lax.axis_size(a) for a in axis) if isinstance(axis, tuple) else lax.axis_size(axis)
    first, last = max(0, -steps), min(count, count - steps)
    return lax.ppermute(value, axis, [(source, source + steps) for source in range(first, last)])


COL = ("layer", "core")
CHIPS = ("layer", "row")


def body(object_field, probe, corners, counts, amplitude):
    layers, rows = lax.axis_size("layer"), lax.axis_size("row")
    tables = [jnp.asarray(table) for table in transform_tables()]
    probe = probe.reshape(2 * MODES, WIN, WIN)
    corners, counts = corners[:, 0, 0], counts[:, 0, 0]
    amplitude = amplitude[:, 0, 0]

    first_cols = object_field[:, :, :WIN]
    below0 = shift(first_cols, "row", -1)
    rim = shift(first_cols, COL, -1)
    first_cols, again = lax.optimization_barrier((first_cols, object_field))
    below1 = shift(again[:, :, WIN:], "row", -1)
    diag = shift(below0, COL, -1)
    rims = (below0, below1, rim, diag)

    def swap(value):
        return lax.ppermute(value, "core", [(0, 1), (1, 0)])

    def reduce_chips(keep, send):
        (value,) = call(add_kernel, [keep, swap(send)], [f32(*keep.shape)], 0, 48)
        parts = lax.all_to_all(value.reshape(layers, rows * CHUNK, HALF), "layer", 0, 0, tiled=True)
        return call(sum_kernel, [parts], [f32(rows * CHUNK, HALF), f32(8, HALF)], 0, 48)

    def reduce_rows(part):
        return lax.all_to_all(part.reshape(rows, CHUNK, HALF), "row", 0, 0, tiled=True)

    def finish_tile(sums, from_left, chunk, loss, loss_before):
        outs = [f32(2, WIN, 2 * WIN), f32(layers * rows, SENT, HALF), f32(1, 2)]
        args = [sums[0], sums[1], from_left, chunk, loss, loss_before]
        tile, sent, losses = call(tile_kernel, args, outs, 0, 48)
        return tile, lax.all_to_all(sent, CHIPS, 0, 0, tiled=True), losses

    def fold(*windows, token):
        both = len(windows) == 3
        strip = f32(1 + both, 2, WIN, WIN)
        return call(lambda *refs: fold_kernel(both, *refs), [*windows, token], [strip] * 3, 0, 48)

    grads, keep, send, loss_first = window_call(
        0, corners, counts, [object_field, *rims, tables[0], probe], amplitude, tables
    )
    down, up = shift(grads, "row", 1), shift(grads, "row", -1)
    part, token = reduce_chips(keep, send)
    sums = fold(grads, down, up, token=token)
    chunk, sums = lax.optimization_barrier((reduce_rows(part), sums))
    from_left, from_right = shift(sums[2], COL, 1), shift(sums[0], COL, -1)
    tile_first, mine, _ = finish_tile(sums, from_left, chunk, loss_first, loss_first)
    patches = call(
        patch_kernel,
        [corners, object_field, *rims, *sums, from_left, from_right],
        [f32(CAP, 2, WIN, WIN)] * 2,
        1,
    )

    mine, patches = lax.optimization_barrier((mine, patches))

    grads, keep, send, probe_mid, rate_first, loss_second = window_call(
        1, corners, counts, [mine, swap(mine), probe, *patches, tables[0]], amplitude, tables
    )
    down = shift(grads, "row", 1)
    part, token = reduce_chips(keep, send)
    sums = fold(grads, down, token=token)
    chunk, sums = lax.optimization_barrier((reduce_rows(part), sums))
    from_left = shift(sums[2], COL, 1)
    tile_second, mine, losses = finish_tile(sums, from_left, chunk, loss_second, loss_first)
    object_out, probe_out = final_call(
        rate_first, [mine, swap(mine), probe_mid, object_field, tile_first, tile_second]
    )
    losses = losses.reshape(1, 1, 2).transpose(2, 0, 1)
    return (object_out, probe_out.reshape(MODES, 2, WIN, WIN), losses)


def solution(mesh):
    rows, cols = mesh.shape["row"], mesh.shape["col"]
    fine = Mesh(mesh.devices.reshape(rows, cols // 2, 2), ("row", "layer", "core"))
    in_specs = (
        P(None, "row", COL),
        P(),
        P(None, "row", COL, None, None),
        P(None, "row", COL),
        P(None, "row", COL, None, None, None),
    )
    out_specs = (P(None, "row", COL), P(), P(None, "row", COL))
    return jax.shard_map(body, mesh=fine, in_specs=in_specs, out_specs=out_specs, check_vma=False)
```

```python
import math

import jax
import jax.numpy as jnp
import numpy as np
from jax import lax
from jax.experimental import pallas as pl
from jax.experimental.pallas import tpu as pltpu
from jax.sharding import Mesh
from jax.sharding import PartitionSpec as P

WIN = 256
HALF = 128
MODES = 3
CAP = 2
AREA = float(WIN * WIN)
CHUNK = 24
INFO = 8
SENT = 32
MEGA = 1024 * 1024
F32 = jnp.float32
SMEM = pl.BlockSpec(memory_space=pltpu.SMEM)
VMEM = pl.BlockSpec(memory_space=pltpu.VMEM)
ANY = pl.BlockSpec(memory_space=pl.ANY)


def f32(*shape):
    return jax.ShapeDtypeStruct(shape, F32)


def split_bf16(value):
    high = value.astype(jnp.bfloat16)
    low = (value - high.astype(F32)).astype(jnp.bfloat16)
    return high, low


def transform_tables():
    freq = np.arange(HALF)[:, None]
    pixel = np.arange(HALF)[None, :]
    tables = []
    for odd in (0, 1):
        angle = -2.0 * math.pi * (((2 * freq + odd) * pixel) % WIN) / WIN
        cos, sin = np.cos(angle) / math.sqrt(WIN), np.sin(angle) / math.sqrt(WIN)
        tables.append(np.block([[cos, -sin], [sin, cos]]).astype(np.float32))
    tables = np.stack([tables[0], tables[1], tables[0].T, tables[1].T])
    high = tables.astype(jnp.bfloat16)
    low = (tables - high.astype(np.float32)).astype(jnp.bfloat16)
    order = np.concatenate([np.arange(0, WIN, 2), np.arange(1, WIN, 2)])
    shuffle = np.zeros((WIN, WIN), np.float32)
    shuffle[np.arange(WIN), order] = 1.0
    return np.stack([high, low], axis=1), np.stack([shuffle, shuffle.T]).astype(jnp.bfloat16)


def product(left, right):
    return jnp.dot(left, right, preferred_element_type=F32)


def left_apply(table_ref, index, data):
    high, low = split_bf16(data)
    table = jnp.concatenate([table_ref[index, 0], table_ref[index, 0], table_ref[index, 1]], axis=1)
    return product(table, jnp.concatenate([high, low, high], axis=0))


def right_apply(lhs, odd, table_ref, index):
    both, high = lhs[odd], lhs[odd, :, :WIN]
    table = jnp.concatenate([table_ref[index, 0], table_ref[index, 0], table_ref[index, 1]], axis=0)
    return product(jnp.concatenate([both, high], axis=1), table)


def row_place(shape=(WIN, WIN)):
    return lax.broadcasted_iota(jnp.int32, shape, 0)


def col_place(shape=(WIN, WIN)):
    return lax.broadcasted_iota(jnp.int32, shape, 1)


def corner_of(corner_ref, iteration, slot):
    row, col = corner_ref[iteration, slot, 0], corner_ref[iteration, slot, 1]
    return lax.rem(row, WIN), lax.rem(col, WIN), lax.rem(lax.div(col, WIN), 2)


def cut(corner, upper, lower):
    row, col, block = corner
    first = row_place() >= row
    blocks = [jnp.where(first, above, below) for above, below in zip(upper, lower)]
    left = jnp.where(block == 0, blocks[0], blocks[1])
    right = jnp.where(block == 0, blocks[1], blocks[2])
    value = jnp.where(col_place() >= col, left, right)
    value = pltpu.roll(value, lax.rem(WIN - row, WIN), 0)
    return pltpu.roll(value, lax.rem(WIN - col, WIN), 1)


def rate_of(mine, other):
    total = jnp.sum(mine[:, CHUNK:], axis=0) + jnp.sum(other[:, CHUNK:], axis=0)
    return total[0:1] / (total[1:2] + 1e-06)


def gathered_plane(half, index):
    pieces, row, end = [], index * WIN, (index + 1) * WIN
    while row < end:
        chunk, offset = divmod(row, CHUNK)
        size = min(CHUNK - offset, end - row)
        pieces.append(half[chunk, offset : offset + size])
        row += size
    return jnp.concatenate(pieces, axis=0)


def probe_step(mine, other, core):
    planes = []
    for plane in range(2 * MODES):
        sides = []
        for side in range(2):
            half, index = divmod(2 * plane + side, 2 * MODES)
            own, swapped = gathered_plane(mine, index), gathered_plane(other, index)
            sides.append(jnp.where(core == half, own, swapped))
        planes.append(jnp.concatenate(sides, axis=1))
    return planes


def window_kernel(iteration, corner_ref, count_ref, *refs):
    refs = list(refs)
    core = lax.axis_index("core")
    n_big = 9 if iteration == 0 else 8
    sources, refs = refs[:n_big], refs[n_big:]
    out_grad, out_keep, out_send = refs[:3]
    refs = refs[3:]
    if iteration:
        out_mid, out_rate = refs[:2]
        refs = refs[2:]
    out_loss, obj, field, lhs, factor, total_probe, grads, sems, out_sems, probe_sems, mid_sem = refs[:11]
    held = refs[11:]
    fetch = [pltpu.make_async_copy(src, dst, sems.at[k]) for k, (src, dst) in enumerate(zip(sources, held))]
    for copy in fetch:
        copy.start()
    if iteration == 0:
        tile, below0, below1, rim, diag, tables, probe_ref, amp_ref, shuffle = held
    else:
        mine, other, probe_ref, patch, patch_grad, tables, amp_ref, shuffle = held
    for copy in fetch[: 5 if iteration == 0 else 3]:
        copy.wait()

    if iteration:
        rate = rate_of(mine, other)
        out_rate[...] = jnp.broadcast_to(rate, (8, HALF))
        wide = jnp.concatenate([rate, rate], axis=1)
        for plane, step in enumerate(probe_step(mine, other, core)):
            probe_ref[plane] = probe_ref[plane] - wide * step
        mid_copy = pltpu.make_async_copy(probe_ref, out_mid, mid_sem.at[0])
        mid_copy.start()

    def deliver(index):
        half, place = divmod(index, 2 * MODES)
        keep = pltpu.make_async_copy(total_probe.at[index], out_keep.at[place], probe_sems.at[index])
        send = pltpu.make_async_copy(total_probe.at[index], out_send.at[place], probe_sems.at[index])
        return half, keep, send

    losses = jnp.zeros((8, HALF), F32)
    for slot in range(CAP):
        corner = corner_of(corner_ref, iteration, slot)
        alive = (slot < count_ref[iteration]).astype(F32)
        if iteration and slot == 0:
            for copy in fetch[3:5]:
                copy.wait()
        for part in range(2):
            if iteration == 0:
                obj[part] = cut(
                    corner,
                    (tile[part, :, :WIN], tile[part, :, WIN:], rim[part]),
                    (below0[part], below1[part], diag[part]),
                )
            else:
                obj[part] = patch[slot, part] - wide * patch_grad[slot, part]

        if slot == 0:
            for copy in fetch[5:-2]:
                copy.wait()
        for mode in range(MODES):
            probe_re, probe_im = probe_ref[2 * mode], probe_ref[2 * mode + 1]
            exit_re = probe_re * obj[0] - probe_im * obj[1]
            exit_im = probe_re * obj[1] + probe_im * obj[0]
            half = []
            for odd in range(2):
                sign = -1.0 if odd else 1.0
                folded = jnp.concatenate(
                    [exit_re[:HALF] + sign * exit_re[HALF:], exit_im[:HALF] + sign * exit_im[HALF:]], axis=0
                )
                half.append(left_apply(tables, odd, folded))
            mid_re = jnp.concatenate([half[0][:HALF], half[1][:HALF]], axis=0)
            mid_im = jnp.concatenate([half[0][HALF:], half[1][HALF:]], axis=0)
            for odd in range(2):
                sign = -1.0 if odd else 1.0
                folded = jnp.concatenate(
                    [mid_re[:, :HALF] + sign * mid_re[:, HALF:], mid_im[:, :HALF] + sign * mid_im[:, HALF:]], axis=1
                )
                high, low = split_bf16(folded)
                rows = slice(mode * WIN, (mode + 1) * WIN)
                lhs[odd, rows, :WIN], lhs[odd, rows, WIN:] = high, low
        for odd in range(2):
            field[odd] = right_apply(lhs, odd, tables, 2 + odd)

        if slot == 0:
            fetch[-2].wait()
            fetch[-1].wait()
        amp = product(shuffle[0], amp_ref[iteration, slot]).astype(jnp.bfloat16)
        amp = product(amp, shuffle[1])
        loss = jnp.zeros((WIN, HALF), F32)
        for odd in range(2):
            total = jnp.ones((WIN, HALF), F32)
            for mode in range(MODES):
                rows = slice(mode * WIN, (mode + 1) * WIN)
                real, imag = field[odd, rows, :HALF], field[odd, rows, HALF:]
                total = total + (real * real + imag * imag)
            inverse = lax.rsqrt(total)
            measured = amp[:, odd * HALF : (odd + 1) * HALF]
            gap = total * inverse - measured
            loss = loss + gap * gap
            factor[odd] = (1.0 - measured * inverse) * (2.0 / AREA * alive)
        losses = losses + jnp.sum(loss.reshape(WIN // 8, 8, HALF), axis=0) * (alive / AREA)

        grad_re = jnp.zeros((WIN, WIN), F32)
        grad_im = jnp.zeros((WIN, WIN), F32)
        for odd in range(2):
            scale = jnp.concatenate([factor[odd], factor[odd]], axis=1)
            for mode in range(MODES):
                rows = slice(mode * WIN, (mode + 1) * WIN)
                high, low = split_bf16(field[odd, rows] * scale)
                lhs[odd, rows, :WIN], lhs[odd, rows, WIN:] = high, low
        for odd in range(2):
            field[odd] = right_apply(lhs, odd, tables, odd)
        for mode in range(MODES):
            half = [field[odd, mode * WIN : (mode + 1) * WIN] for odd in range(2)]
            mid_re = jnp.concatenate(
                [half[0][:, :HALF] + half[1][:, :HALF], half[0][:, :HALF] - half[1][:, :HALF]], axis=1
            )
            mid_im = jnp.concatenate(
                [half[0][:, HALF:] + half[1][:, HALF:], half[0][:, HALF:] - half[1][:, HALF:]], axis=1
            )
            back = []
            for odd in range(2):
                rows = slice(odd * HALF, (odd + 1) * HALF)
                back.append(left_apply(tables, 2 + odd, jnp.concatenate([mid_re[rows], mid_im[rows]], axis=0)))
            back_re = jnp.concatenate([back[0][:HALF] + back[1][:HALF], back[0][:HALF] - back[1][:HALF]], axis=0)
            back_im = jnp.concatenate([back[0][HALF:] + back[1][HALF:], back[0][HALF:] - back[1][HALF:]], axis=0)
            probe_re, probe_im = probe_ref[2 * mode], probe_ref[2 * mode + 1]
            grad_re = grad_re + (probe_re * back_re + probe_im * back_im)
            grad_im = grad_im + (probe_re * back_im - probe_im * back_re)
            terms = (obj[0] * back_re + obj[1] * back_im, obj[0] * back_im - obj[1] * back_re)
            for part in range(2):
                for side in range(2):
                    index = (2 * mode + part) * 2 + side
                    value = terms[part][:, side * HALF : (side + 1) * HALF]
                    if slot:
                        value = value + total_probe[index]
                    total_probe[index] = value
                    if slot:
                        half, keep, send = deliver(index)
                        pl.when(core == half)(keep.start)
                        pl.when(core != half)(send.start)
        for part, value in enumerate((grad_re, grad_im)):
            grads[slot, part, :WIN] = pltpu.roll(pltpu.roll(value, corner[0], 0), corner[1], 1)
            row = row_place((INFO, WIN))
            info = jnp.where(row == 0, corner[0], jnp.where(row == 1, corner[1], corner[2]))
            grads[slot, part, WIN:] = info.astype(F32)
        pltpu.make_async_copy(grads.at[slot], out_grad.at[slot], out_sems.at[slot]).start()
    out_loss[...] = losses
    for index in range(4 * MODES):
        half, keep, send = deliver(index)
        pl.when(core == half)(keep.wait)
        pl.when(core != half)(send.wait)
    for slot in range(CAP):
        pltpu.make_async_copy(grads.at[slot], out_grad.at[slot], out_sems.at[slot]).wait()
    if iteration:
        mid_copy.wait()


def call(kernel, args, out_shape, n_smem, limit=60):
    size = sum(math.prod(a.shape) * a.dtype.itemsize for a in (*args, *out_shape))
    return pl.pallas_call(
        kernel,
        out_shape=tuple(out_shape),
        in_specs=[SMEM] * n_smem + [VMEM] * (len(args) - n_smem),
        out_specs=tuple([VMEM] * len(out_shape)),
        compiler_params=pltpu.CompilerParams(vmem_limit_bytes=limit * MEGA),
        cost_estimate=pl.CostEstimate(flops=10_000_000, bytes_accessed=size, transcendentals=0),
    )(*args)


def window_call(iteration, corners, counts, data, amplitude, tables):
    outs = [f32(CAP, 2, WIN + INFO, WIN), f32(2 * MODES, WIN, HALF), f32(2 * MODES, WIN, HALF)]
    out_specs = [ANY] * 3
    if iteration:
        outs += [f32(2 * MODES, WIN, WIN), f32(8, HALF)]
        out_specs += [ANY, VMEM]
    big = [*data, amplitude, tables[1]]
    return pl.pallas_call(
        lambda *refs: window_kernel(iteration, *refs),
        out_shape=(*outs, f32(8, HALF)),
        in_specs=[SMEM] * 2 + [ANY] * len(big),
        out_specs=(*out_specs, VMEM),
        scratch_shapes=[
            pltpu.VMEM((2, WIN, WIN), F32),
            pltpu.VMEM((2, MODES * WIN, WIN), F32),
            pltpu.VMEM((2, MODES * WIN, 2 * WIN), jnp.bfloat16),
            pltpu.VMEM((2, WIN, HALF), F32),
            pltpu.VMEM((4 * MODES, WIN, HALF), F32),
            pltpu.VMEM((CAP, 2, WIN + INFO, WIN), F32),
            pltpu.SemaphoreType.DMA((len(big),)),
            pltpu.SemaphoreType.DMA((CAP,)),
            pltpu.SemaphoreType.DMA((4 * MODES,)),
            pltpu.SemaphoreType.DMA((1,)),
            *[pltpu.VMEM(value.shape, value.dtype) for value in big],
        ],
        compiler_params=pltpu.CompilerParams(vmem_limit_bytes=48 * MEGA),
        cost_estimate=pl.CostEstimate(flops=8_000_000_000, bytes_accessed=12_000_000, transcendentals=0),
    )(corners, counts, *big)


def fold_kernel(both, *refs):
    *refs, token, out0, out1, out2 = refs
    outs = (out0, out1, out2)
    rows, cols = row_place(), col_place((1, WIN))
    masks = []
    for windows in refs:
        for slot in range(CAP):
            info = windows[slot, 0, WIN:].astype(jnp.int32)
            masks.append((rows >= info[0:1], jnp.where(cols >= info[1:2], info[2:3], info[2:3] + 1)))
    for part in range(2):
        top, bottom = [0.0] * 3, [0.0] * 3
        for which, windows in enumerate(refs):
            for slot in range(CAP):
                first, target = masks[which * CAP + slot]
                window = windows[slot, part, :WIN]
                upper = jnp.where(first, window, 0.0) if which != 1 else None
                lower = jnp.where(first, 0.0, window) if which != 2 else None
                for index in range(3):
                    here = target == index
                    if which == 0:
                        top[index] += jnp.where(here, upper, 0.0)
                        if both:
                            bottom[index] += jnp.where(here, lower, 0.0)
                    elif which == 1:
                        top[index] += jnp.where(here, lower, 0.0)
                    else:
                        bottom[index] += jnp.where(here, upper, 0.0)
        for index in range(3):
            outs[index][0, part] = top[index]
            if both:
                outs[index][1, part] = bottom[index]
    outs[0][0, 0, :8, :HALF] = outs[0][0, 0, :8, :HALF] + token[...]


def add_kernel(keep, other, out):
    out[...] = keep[...] + other[...]


def sum_kernel(parts, out, out_token):
    out[...] = jnp.sum(parts[...], axis=0)
    out_token[...] = jnp.zeros_like(out_token)


def tile_kernel(block0, block1, from_left, parts, loss, loss_before, out_tile, out_sent, out_loss):
    chunk = jnp.sum(parts[...], axis=0)
    square = sum(chunk[k : k + 8] * chunk[k : k + 8] for k in range(0, CHUNK, 8))
    for part in range(2):
        values = (block0[0, part] + from_left[0, part], block1[0, part])
        for index, value in enumerate(values):
            out_tile[part, :, index * WIN : (index + 1) * WIN] = value
            pieces = jnp.sum((value * value).reshape(WIN // 8, 8, WIN), axis=0)
            square = square + (pieces[:, :HALF] + pieces[:, HALF:])
    loss = jnp.sum(loss[...])
    out_loss[...] = jnp.where(col_place((1, 2)) == 0, jnp.sum(loss_before[...]), loss)
    scalars = jnp.where(row_place((SENT - CHUNK, HALF)) == 0, loss, jnp.sum(square))
    value = jnp.concatenate([chunk, scalars], axis=0)
    for index in range(out_sent.shape[0]):
        out_sent[index] = value


def patch_kernel(corner_ref, tile, below0, below1, rim, diag, block0, block1, block2, left, right, out_obj, out_grad):
    for part in range(2):
        upper = (tile[part, :, :WIN], tile[part, :, WIN:], rim[part])
        lower = (below0[part], below1[part], diag[part])
        grad = [
            (block0[k, part] + left[k, part], block1[k, part], block2[k, part] + right[k, part]) for k in range(2)
        ]
        for slot in range(CAP):
            corner = corner_of(corner_ref, 1, slot)
            out_obj[slot, part] = cut(corner, upper, lower)
            out_grad[slot, part] = cut(corner, grad[0], grad[1])


def final_kernel(rate_first, *refs):
    sources, (out_tile, out_probe) = refs[:6], refs[6:8]
    held, (new_tile, new_probe), sems, tile_sems, probe_sems = refs[8:14], refs[14:16], *refs[16:]
    fetch = [pltpu.make_async_copy(src, dst, sems.at[k]) for k, (src, dst) in enumerate(zip(sources, held))]
    for copy in fetch:
        copy.start()
    mine, other, probe, tile, grad_first, grad_second = held
    core = lax.axis_index("core")
    for copy in fetch[:3]:
        copy.wait()
    rate = rate_of(mine, other)
    wide = jnp.concatenate([rate, rate], axis=1)
    back = []
    for plane, step in enumerate(probe_step(mine, other, core)):
        new_probe[plane] = probe[plane] - wide * step
        back.append(pltpu.make_async_copy(new_probe.at[plane], out_probe.at[plane], probe_sems.at[plane]))
        back[-1].start()
    for copy in fetch[3:]:
        copy.wait()
    first = jnp.concatenate([rate_first[0:1]] * 4, axis=1)
    second = jnp.concatenate([rate] * 4, axis=1)
    for part in range(2):
        new_tile[part] = (tile[part] - first * grad_first[part]) - second * grad_second[part]
        back.append(pltpu.make_async_copy(new_tile.at[part], out_tile.at[part], tile_sems.at[part]))
        back[-1].start()
    for copy in back:
        copy.wait()


def final_call(rate_first, data):
    outs = (f32(2, WIN, 2 * WIN), f32(2 * MODES, WIN, WIN))
    return pl.pallas_call(
        final_kernel,
        out_shape=outs,
        in_specs=[VMEM] + [ANY] * len(data),
        out_specs=(ANY, ANY),
        scratch_shapes=[
            *[pltpu.VMEM(value.shape, value.dtype) for value in (*data, *outs)],
            pltpu.SemaphoreType.DMA((len(data),)),
            pltpu.SemaphoreType.DMA((2,)),
            pltpu.SemaphoreType.DMA((2 * MODES,)),
        ],
        compiler_params=pltpu.CompilerParams(vmem_limit_bytes=48 * MEGA),
        cost_estimate=pl.CostEstimate(flops=10_000_000, bytes_accessed=9_000_000, transcendentals=0),
    )(rate_first, *data)


def shift(value, axis, steps):
    count = math.prod(lax.axis_size(a) for a in axis) if isinstance(axis, tuple) else lax.axis_size(axis)
    first, last = max(0, -steps), min(count, count - steps)
    return lax.ppermute(value, axis, [(source, source + steps) for source in range(first, last)])


COL = ("layer", "core")
CHIPS = ("layer", "row")


def body(object_field, probe, corners, counts, amplitude):
    layers, rows = lax.axis_size("layer"), lax.axis_size("row")
    tables = [jnp.asarray(table) for table in transform_tables()]
    probe = probe.reshape(2 * MODES, WIN, WIN)
    corners, counts = corners[:, 0, 0], counts[:, 0, 0]
    amplitude = amplitude[:, 0, 0]

    first_cols = object_field[:, :, :WIN]
    below0 = shift(first_cols, "row", -1)
    rim = shift(first_cols, COL, -1)
    first_cols, again = lax.optimization_barrier((first_cols, object_field))
    below1 = shift(again[:, :, WIN:], "row", -1)
    diag = shift(below0, COL, -1)
    rims = (below0, below1, rim, diag)

    def swap(value):
        return lax.ppermute(value, "core", [(0, 1), (1, 0)])

    def reduce_chips(keep, send):
        (value,) = call(add_kernel, [keep, swap(send)], [f32(*keep.shape)], 0, 48)
        parts = lax.all_to_all(value.reshape(layers, rows * CHUNK, HALF), "layer", 0, 0, tiled=True)
        return call(sum_kernel, [parts], [f32(rows * CHUNK, HALF), f32(8, HALF)], 0, 48)

    def reduce_rows(part):
        return lax.all_to_all(part.reshape(rows, CHUNK, HALF), "row", 0, 0, tiled=True)

    def finish_tile(sums, from_left, chunk, loss, loss_before):
        outs = [f32(2, WIN, 2 * WIN), f32(layers * rows, SENT, HALF), f32(1, 2)]
        args = [sums[0], sums[1], from_left, chunk, loss, loss_before]
        tile, sent, losses = call(tile_kernel, args, outs, 0, 48)
        return tile, lax.all_to_all(sent, CHIPS, 0, 0, tiled=True), losses

    def fold(*windows, token):
        both = len(windows) == 3
        strip = f32(1 + both, 2, WIN, WIN)
        return call(lambda *refs: fold_kernel(both, *refs), [*windows, token], [strip] * 3, 0, 48)

    grads, keep, send, loss_first = window_call(
        0, corners, counts, [object_field, *rims, tables[0], probe], amplitude, tables
    )
    down, up = shift(grads, "row", 1), shift(grads, "row", -1)
    part, token = reduce_chips(keep, send)
    sums = fold(grads, down, up, token=token)
    chunk, sums = lax.optimization_barrier((reduce_rows(part), sums))
    from_left, from_right = shift(sums[2], COL, 1), shift(sums[0], COL, -1)
    tile_first, mine, _ = finish_tile(sums, from_left, chunk, loss_first, loss_first)
    patches = call(
        patch_kernel,
        [corners, object_field, *rims, *sums, from_left, from_right],
        [f32(CAP, 2, WIN, WIN)] * 2,
        1,
    )

    mine, patches = lax.optimization_barrier((mine, patches))

    grads, keep, send, probe_mid, rate_first, loss_second = window_call(
        1, corners, counts, [mine, swap(mine), probe, *patches, tables[0]], amplitude, tables
    )
    down = shift(grads, "row", 1)
    part, token = reduce_chips(keep, send)
    sums = fold(grads, down, token=token)
    chunk, sums = lax.optimization_barrier((reduce_rows(part), sums))
    from_left = shift(sums[2], COL, 1)
    tile_second, mine, losses = finish_tile(sums, from_left, chunk, loss_second, loss_first)
    object_out, probe_out = final_call(
        rate_first, [mine, swap(mine), probe_mid, object_field, tile_first, tile_second]
    )
    losses = losses.reshape(1, 1, 2).transpose(2, 0, 1)
    return (object_out, probe_out.reshape(MODES, 2, WIN, WIN), losses)


def solution(mesh):
    rows, cols = mesh.shape["row"], mesh.shape["col"]
    fine = Mesh(mesh.devices.reshape(rows, cols // 2, 2), ("row", "layer", "core"))
    in_specs = (
        P(None, "row", COL),
        P(),
        P(None, "row", COL, None, None),
        P(None, "row", COL),
        P(None, "row", COL, None, None, None),
    )
    out_specs = (P(None, "row", COL), P(), P(None, "row", COL))
    return jax.shard_map(body, mesh=fine, in_specs=in_specs, out_specs=out_specs, check_vma=False)
```

```python
import math

import jax
import jax.numpy as jnp
import numpy as np
from jax import lax
from jax.experimental import pallas as pl
from jax.experimental.pallas import tpu as pltpu
from jax.sharding import Mesh
from jax.sharding import PartitionSpec as P

WIN = 256
HALF = 128
MODES = 3
CAP = 2
AREA = float(WIN * WIN)
CHUNK = 24
INFO = 8
SENT = 32
MEGA = 1024 * 1024
F32 = jnp.float32
SMEM = pl.BlockSpec(memory_space=pltpu.SMEM)
VMEM = pl.BlockSpec(memory_space=pltpu.VMEM)
ANY = pl.BlockSpec(memory_space=pl.ANY)


def f32(*shape):
    return jax.ShapeDtypeStruct(shape, F32)


def split_bf16(value):
    high = value.astype(jnp.bfloat16)
    low = (value - high.astype(F32)).astype(jnp.bfloat16)
    return high, low


def transform_tables():
    freq = np.arange(HALF)[:, None]
    pixel = np.arange(HALF)[None, :]
    tables = []
    for odd in (0, 1):
        angle = -2.0 * math.pi * (((2 * freq + odd) * pixel) % WIN) / WIN
        cos, sin = np.cos(angle) / math.sqrt(WIN), np.sin(angle) / math.sqrt(WIN)
        tables.append(np.block([[cos, -sin], [sin, cos]]).astype(np.float32))
    tables = np.stack([tables[0], tables[1], tables[0].T, tables[1].T])
    high = tables.astype(jnp.bfloat16)
    low = (tables - high.astype(np.float32)).astype(jnp.bfloat16)
    order = np.concatenate([np.arange(0, WIN, 2), np.arange(1, WIN, 2)])
    shuffle = np.zeros((WIN, WIN), np.float32)
    shuffle[np.arange(WIN), order] = 1.0
    return np.stack([high, low], axis=1), np.stack([shuffle, shuffle.T]).astype(jnp.bfloat16)


def product(left, right):
    return jnp.dot(left, right, preferred_element_type=F32)


def left_apply(table_ref, index, data):
    high, low = split_bf16(data)
    table = jnp.concatenate([table_ref[index, 0], table_ref[index, 0], table_ref[index, 1]], axis=1)
    return product(table, jnp.concatenate([high, low, high], axis=0))


def right_apply(lhs, odd, table_ref, index):
    both, high = lhs[odd], lhs[odd, :, :WIN]
    table = jnp.concatenate([table_ref[index, 0], table_ref[index, 0], table_ref[index, 1]], axis=0)
    return product(jnp.concatenate([both, high], axis=1), table)


def row_place(shape=(WIN, WIN)):
    return lax.broadcasted_iota(jnp.int32, shape, 0)


def col_place(shape=(WIN, WIN)):
    return lax.broadcasted_iota(jnp.int32, shape, 1)


def corner_of(corner_ref, iteration, slot):
    row, col = corner_ref[iteration, slot, 0], corner_ref[iteration, slot, 1]
    return lax.rem(row, WIN), lax.rem(col, WIN), lax.rem(lax.div(col, WIN), 2)


def cut(corner, upper, lower):
    row, col, block = corner
    first = row_place() >= row
    blocks = [jnp.where(first, above, below) for above, below in zip(upper, lower)]
    left = jnp.where(block == 0, blocks[0], blocks[1])
    right = jnp.where(block == 0, blocks[1], blocks[2])
    value = jnp.where(col_place() >= col, left, right)
    value = pltpu.roll(value, lax.rem(WIN - row, WIN), 0)
    return pltpu.roll(value, lax.rem(WIN - col, WIN), 1)


def rate_of(mine, other):
    total = jnp.sum(mine[:, CHUNK:], axis=0) + jnp.sum(other[:, CHUNK:], axis=0)
    return total[0:1] / (total[1:2] + 1e-06)


def gathered_plane(half, index):
    pieces, row, end = [], index * WIN, (index + 1) * WIN
    while row < end:
        chunk, offset = divmod(row, CHUNK)
        size = min(CHUNK - offset, end - row)
        pieces.append(half[chunk, offset : offset + size])
        row += size
    return jnp.concatenate(pieces, axis=0)


def probe_step(mine, other, core):
    planes = []
    for plane in range(2 * MODES):
        sides = []
        for side in range(2):
            half, index = divmod(2 * plane + side, 2 * MODES)
            own, swapped = gathered_plane(mine, index), gathered_plane(other, index)
            sides.append(jnp.where(core == half, own, swapped))
        planes.append(jnp.concatenate(sides, axis=1))
    return planes


def window_kernel(iteration, corner_ref, count_ref, *refs):
    refs = list(refs)
    core = lax.axis_index("core")
    n_big = 9 if iteration == 0 else 8
    sources, refs = refs[:n_big], refs[n_big:]
    out_grad, out_keep, out_send = refs[:3]
    refs = refs[3:]
    if iteration:
        out_mid, out_rate = refs[:2]
        refs = refs[2:]
    out_loss, obj, field, lhs, factor, total_probe, grads, sems, out_sems, probe_sems, mid_sem = refs[:11]
    direct = 5 if iteration == 0 else 0
    held = [*sources[:direct], *refs[11:]]
    fetch = [pltpu.make_async_copy(src, dst, sems.at[k]) for k, (src, dst) in enumerate(zip(sources[direct:], refs[11:]))]
    for copy in fetch:
        copy.start()
    fetch = [None] * direct + fetch
    if iteration == 0:
        tile, below0, below1, rim, diag, tables, probe_ref, amp_ref, shuffle = held
    else:
        mine, other, probe_ref, patch, patch_grad, tables, amp_ref, shuffle = held
    for copy in fetch[direct : 5 if iteration == 0 else 3]:
        copy.wait()

    if iteration:
        rate = rate_of(mine, other)
        out_rate[...] = jnp.broadcast_to(rate, (8, HALF))
        wide = jnp.concatenate([rate, rate], axis=1)
        for plane, step in enumerate(probe_step(mine, other, core)):
            probe_ref[plane] = probe_ref[plane] - wide * step
        mid_copy = pltpu.make_async_copy(probe_ref, out_mid, mid_sem.at[0])
        mid_copy.start()

    def deliver(index):
        half, place = divmod(index, 2 * MODES)
        keep = pltpu.make_async_copy(total_probe.at[index], out_keep.at[place], probe_sems.at[index])
        send = pltpu.make_async_copy(total_probe.at[index], out_send.at[place], probe_sems.at[index])
        return half, keep, send

    losses = jnp.zeros((8, HALF), F32)
    for slot in range(CAP):
        corner = corner_of(corner_ref, iteration, slot)
        alive = (slot < count_ref[iteration]).astype(F32)
        if iteration and slot == 0:
            for copy in fetch[3:5]:
                copy.wait()
        for part in range(2):
            if iteration == 0:
                obj[part] = cut(
                    corner,
                    (tile[part, :, :WIN], tile[part, :, WIN:], rim[part]),
                    (below0[part], below1[part], diag[part]),
                )
            else:
                obj[part] = patch[slot, part] - wide * patch_grad[slot, part]

        if slot == 0:
            for copy in fetch[5:-2]:
                copy.wait()
        for mode in range(MODES):
            probe_re, probe_im = probe_ref[2 * mode], probe_ref[2 * mode + 1]
            exit_re = probe_re * obj[0] - probe_im * obj[1]
            exit_im = probe_re * obj[1] + probe_im * obj[0]
            half = []
            for odd in range(2):
                sign = -1.0 if odd else 1.0
                folded = jnp.concatenate(
                    [exit_re[:HALF] + sign * exit_re[HALF:], exit_im[:HALF] + sign * exit_im[HALF:]], axis=0
                )
                half.append(left_apply(tables, odd, folded))
            mid_re = jnp.concatenate([half[0][:HALF], half[1][:HALF]], axis=0)
            mid_im = jnp.concatenate([half[0][HALF:], half[1][HALF:]], axis=0)
            for odd in range(2):
                sign = -1.0 if odd else 1.0
                folded = jnp.concatenate(
                    [mid_re[:, :HALF] + sign * mid_re[:, HALF:], mid_im[:, :HALF] + sign * mid_im[:, HALF:]], axis=1
                )
                high, low = split_bf16(folded)
                rows = slice(mode * WIN, (mode + 1) * WIN)
                lhs[odd, rows, :WIN], lhs[odd, rows, WIN:] = high, low
        for odd in range(2):
            field[odd] = right_apply(lhs, odd, tables, 2 + odd)

        if slot == 0:
            fetch[-2].wait()
            fetch[-1].wait()
        amp = product(shuffle[0], amp_ref[iteration, slot]).astype(jnp.bfloat16)
        amp = product(amp, shuffle[1])
        loss = jnp.zeros((WIN, HALF), F32)
        for odd in range(2):
            total = jnp.ones((WIN, HALF), F32)
            for mode in range(MODES):
                rows = slice(mode * WIN, (mode + 1) * WIN)
                real, imag = field[odd, rows, :HALF], field[odd, rows, HALF:]
                total = total + (real * real + imag * imag)
            inverse = lax.rsqrt(total)
            measured = amp[:, odd * HALF : (odd + 1) * HALF]
            gap = total * inverse - measured
            loss = loss + gap * gap
            factor[odd] = (1.0 - measured * inverse) * (2.0 / AREA * alive)
        losses = losses + jnp.sum(loss.reshape(WIN // 8, 8, HALF), axis=0) * (alive / AREA)

        grad_re = jnp.zeros((WIN, WIN), F32)
        grad_im = jnp.zeros((WIN, WIN), F32)
        for odd in range(2):
            scale = jnp.concatenate([factor[odd], factor[odd]], axis=1)
            for mode in range(MODES):
                rows = slice(mode * WIN, (mode + 1) * WIN)
                high, low = split_bf16(field[odd, rows] * scale)
                lhs[odd, rows, :WIN], lhs[odd, rows, WIN:] = high, low
        for odd in range(2):
            field[odd] = right_apply(lhs, odd, tables, odd)
        for mode in range(MODES):
            half = [field[odd, mode * WIN : (mode + 1) * WIN] for odd in range(2)]
            mid_re = jnp.concatenate(
                [half[0][:, :HALF] + half[1][:, :HALF], half[0][:, :HALF] - half[1][:, :HALF]], axis=1
            )
            mid_im = jnp.concatenate(
                [half[0][:, HALF:] + half[1][:, HALF:], half[0][:, HALF:] - half[1][:, HALF:]], axis=1
            )
            back = []
            for odd in range(2):
                rows = slice(odd * HALF, (odd + 1) * HALF)
                back.append(left_apply(tables, 2 + odd, jnp.concatenate([mid_re[rows], mid_im[rows]], axis=0)))
            back_re = jnp.concatenate([back[0][:HALF] + back[1][:HALF], back[0][:HALF] - back[1][:HALF]], axis=0)
            back_im = jnp.concatenate([back[0][HALF:] + back[1][HALF:], back[0][HALF:] - back[1][HALF:]], axis=0)
            probe_re, probe_im = probe_ref[2 * mode], probe_ref[2 * mode + 1]
            grad_re = grad_re + (probe_re * back_re + probe_im * back_im)
            grad_im = grad_im + (probe_re * back_im - probe_im * back_re)
            terms = (obj[0] * back_re + obj[1] * back_im, obj[0] * back_im - obj[1] * back_re)
            for part in range(2):
                for side in range(2):
                    index = (2 * mode + part) * 2 + side
                    value = terms[part][:, side * HALF : (side + 1) * HALF]
                    if slot:
                        value = value + total_probe[index]
                    total_probe[index] = value
                    if slot:
                        half, keep, send = deliver(index)
                        pl.when(core == half)(keep.start)
                        pl.when(core != half)(send.start)
        for part, value in enumerate((grad_re, grad_im)):
            grads[slot, part, :WIN] = pltpu.roll(pltpu.roll(value, corner[0], 0), corner[1], 1)
            row = row_place((INFO, WIN))
            info = jnp.where(row == 0, corner[0], jnp.where(row == 1, corner[1], corner[2]))
            grads[slot, part, WIN:] = info.astype(F32)
        pltpu.make_async_copy(grads.at[slot], out_grad.at[slot], out_sems.at[slot]).start()
    out_loss[...] = losses
    for index in range(4 * MODES):
        half, keep, send = deliver(index)
        pl.when(core == half)(keep.wait)
        pl.when(core != half)(send.wait)
    for slot in range(CAP):
        pltpu.make_async_copy(grads.at[slot], out_grad.at[slot], out_sems.at[slot]).wait()
    if iteration:
        mid_copy.wait()


def call(kernel, args, out_shape, n_smem, limit=60):
    size = sum(math.prod(a.shape) * a.dtype.itemsize for a in (*args, *out_shape))
    return pl.pallas_call(
        kernel,
        out_shape=tuple(out_shape),
        in_specs=[SMEM] * n_smem + [VMEM] * (len(args) - n_smem),
        out_specs=tuple([VMEM] * len(out_shape)),
        compiler_params=pltpu.CompilerParams(vmem_limit_bytes=limit * MEGA),
        cost_estimate=pl.CostEstimate(flops=10_000_000, bytes_accessed=size, transcendentals=0),
    )(*args)


def window_call(iteration, corners, counts, data, amplitude, tables):
    outs = [f32(CAP, 2, WIN + INFO, WIN), f32(2 * MODES, WIN, HALF), f32(2 * MODES, WIN, HALF)]
    out_specs = [ANY] * 3
    if iteration:
        outs += [f32(2 * MODES, WIN, WIN), f32(8, HALF)]
        out_specs += [ANY, VMEM]
    big = [*data, amplitude, tables[1]]
    direct = 5 if iteration == 0 else 0
    return pl.pallas_call(
        lambda *refs: window_kernel(iteration, *refs),
        out_shape=(*outs, f32(8, HALF)),
        in_specs=[SMEM] * 2 + [VMEM] * direct + [ANY] * (len(big) - direct),
        out_specs=(*out_specs, VMEM),
        scratch_shapes=[
            pltpu.VMEM((2, WIN, WIN), F32),
            pltpu.VMEM((2, MODES * WIN, WIN), F32),
            pltpu.VMEM((2, MODES * WIN, 2 * WIN), jnp.bfloat16),
            pltpu.VMEM((2, WIN, HALF), F32),
            pltpu.VMEM((4 * MODES, WIN, HALF), F32),
            pltpu.VMEM((CAP, 2, WIN + INFO, WIN), F32),
            pltpu.SemaphoreType.DMA((len(big),)),
            pltpu.SemaphoreType.DMA((CAP,)),
            pltpu.SemaphoreType.DMA((4 * MODES,)),
            pltpu.SemaphoreType.DMA((1,)),
            *[pltpu.VMEM(value.shape, value.dtype) for value in big[direct:]],
        ],
        compiler_params=pltpu.CompilerParams(vmem_limit_bytes=(60 if iteration else 48) * MEGA),
        cost_estimate=pl.CostEstimate(flops=8_000_000_000, bytes_accessed=12_000_000, transcendentals=0),
    )(corners, counts, *big)


def fold_kernel(both, *refs):
    *refs, token, out0, out1, out2 = refs
    outs = (out0, out1, out2)
    rows, cols = row_place(), col_place((1, WIN))
    masks = []
    for windows in refs:
        for slot in range(CAP):
            info = windows[slot, 0, WIN:].astype(jnp.int32)
            masks.append((rows >= info[0:1], jnp.where(cols >= info[1:2], info[2:3], info[2:3] + 1)))
    for part in range(2):
        top, bottom = [0.0] * 3, [0.0] * 3
        for which, windows in enumerate(refs):
            for slot in range(CAP):
                first, target = masks[which * CAP + slot]
                window = windows[slot, part, :WIN]
                upper = jnp.where(first, window, 0.0) if which != 1 else None
                lower = jnp.where(first, 0.0, window) if which != 2 else None
                for index in range(3):
                    here = target == index
                    if which == 0:
                        top[index] += jnp.where(here, upper, 0.0)
                        if both:
                            bottom[index] += jnp.where(here, lower, 0.0)
                    elif which == 1:
                        top[index] += jnp.where(here, lower, 0.0)
                    else:
                        bottom[index] += jnp.where(here, upper, 0.0)
        for index in range(3):
            outs[index][0, part] = top[index]
            if both:
                outs[index][1, part] = bottom[index]
    outs[0][0, 0, :8, :HALF] = outs[0][0, 0, :8, :HALF] + token[...]


def add_kernel(keep, other, out):
    out[...] = keep[...] + other[...]


def sum_kernel(parts, out, out_token):
    out[...] = jnp.sum(parts[...], axis=0)
    out_token[...] = jnp.zeros_like(out_token)


def tile_kernel(block0, block1, from_left, parts, loss, loss_before, out_tile, out_sent, out_loss):
    chunk = jnp.sum(parts[...], axis=0)
    square = sum(chunk[k : k + 8] * chunk[k : k + 8] for k in range(0, CHUNK, 8))
    for part in range(2):
        values = (block0[0, part] + from_left[0, part], block1[0, part])
        for index, value in enumerate(values):
            out_tile[part, :, index * WIN : (index + 1) * WIN] = value
            pieces = jnp.sum((value * value).reshape(WIN // 8, 8, WIN), axis=0)
            square = square + (pieces[:, :HALF] + pieces[:, HALF:])
    loss = jnp.sum(loss[...])
    out_loss[...] = jnp.where(col_place((1, 2)) == 0, jnp.sum(loss_before[...]), loss)
    scalars = jnp.where(row_place((SENT - CHUNK, HALF)) == 0, loss, jnp.sum(square))
    value = jnp.concatenate([chunk, scalars], axis=0)
    for index in range(out_sent.shape[0]):
        out_sent[index] = value


def patch_kernel(corner_ref, tile, below0, below1, rim, diag, block0, block1, block2, left, right, out_obj, out_grad):
    for part in range(2):
        upper = (tile[part, :, :WIN], tile[part, :, WIN:], rim[part])
        lower = (below0[part], below1[part], diag[part])
        grad = [
            (block0[k, part] + left[k, part], block1[k, part], block2[k, part] + right[k, part]) for k in range(2)
        ]
        for slot in range(CAP):
            corner = corner_of(corner_ref, 1, slot)
            out_obj[slot, part] = cut(corner, upper, lower)
            out_grad[slot, part] = cut(corner, grad[0], grad[1])


def final_kernel(rate_first, *refs):
    sources, (out_tile, out_probe) = refs[:6], refs[6:8]
    held, (new_tile, new_probe), sems, tile_sems, probe_sems = refs[8:14], refs[14:16], *refs[16:]
    fetch = [pltpu.make_async_copy(src, dst, sems.at[k]) for k, (src, dst) in enumerate(zip(sources, held))]
    for copy in fetch:
        copy.start()
    mine, other, probe, tile, grad_first, grad_second = held
    core = lax.axis_index("core")
    for copy in fetch[:3]:
        copy.wait()
    rate = rate_of(mine, other)
    wide = jnp.concatenate([rate, rate], axis=1)
    back = []
    for plane, step in enumerate(probe_step(mine, other, core)):
        new_probe[plane] = probe[plane] - wide * step
        back.append(pltpu.make_async_copy(new_probe.at[plane], out_probe.at[plane], probe_sems.at[plane]))
        back[-1].start()
    for copy in fetch[3:]:
        copy.wait()
    first = jnp.concatenate([rate_first[0:1]] * 4, axis=1)
    second = jnp.concatenate([rate] * 4, axis=1)
    for part in range(2):
        new_tile[part] = (tile[part] - first * grad_first[part]) - second * grad_second[part]
        back.append(pltpu.make_async_copy(new_tile.at[part], out_tile.at[part], tile_sems.at[part]))
        back[-1].start()
    for copy in back:
        copy.wait()


def final_call(rate_first, data):
    outs = (f32(2, WIN, 2 * WIN), f32(2 * MODES, WIN, WIN))
    return pl.pallas_call(
        final_kernel,
        out_shape=outs,
        in_specs=[VMEM] + [ANY] * len(data),
        out_specs=(ANY, ANY),
        scratch_shapes=[
            *[pltpu.VMEM(value.shape, value.dtype) for value in (*data, *outs)],
            pltpu.SemaphoreType.DMA((len(data),)),
            pltpu.SemaphoreType.DMA((2,)),
            pltpu.SemaphoreType.DMA((2 * MODES,)),
        ],
        compiler_params=pltpu.CompilerParams(vmem_limit_bytes=48 * MEGA),
        cost_estimate=pl.CostEstimate(flops=10_000_000, bytes_accessed=9_000_000, transcendentals=0),
    )(rate_first, *data)


def shift(value, axis, steps):
    count = math.prod(lax.axis_size(a) for a in axis) if isinstance(axis, tuple) else lax.axis_size(axis)
    first, last = max(0, -steps), min(count, count - steps)
    return lax.ppermute(value, axis, [(source, source + steps) for source in range(first, last)])


COL = ("layer", "core")
CHIPS = ("layer", "row")


def body(object_field, probe, corners, counts, amplitude):
    layers, rows = lax.axis_size("layer"), lax.axis_size("row")
    tables = [jnp.asarray(table) for table in transform_tables()]
    probe = probe.reshape(2 * MODES, WIN, WIN)
    corners, counts = corners[:, 0, 0], counts[:, 0, 0]
    amplitude = amplitude[:, 0, 0]

    first_cols = object_field[:, :, :WIN]
    below0 = shift(first_cols, "row", -1)
    rim = shift(first_cols, COL, -1)
    first_cols, again = lax.optimization_barrier((first_cols, object_field))
    below1 = shift(again[:, :, WIN:], "row", -1)
    diag = shift(below0, COL, -1)
    rims = (below0, below1, rim, diag)

    def swap(value):
        return lax.ppermute(value, "core", [(0, 1), (1, 0)])

    def reduce_chips(keep, send):
        (value,) = call(add_kernel, [keep, swap(send)], [f32(*keep.shape)], 0, 48)
        parts = lax.all_to_all(value.reshape(layers, rows * CHUNK, HALF), "layer", 0, 0, tiled=True)
        return call(sum_kernel, [parts], [f32(rows * CHUNK, HALF), f32(8, HALF)], 0, 48)

    def reduce_rows(part):
        return lax.all_to_all(part.reshape(rows, CHUNK, HALF), "row", 0, 0, tiled=True)

    def finish_tile(sums, from_left, chunk, loss, loss_before):
        outs = [f32(2, WIN, 2 * WIN), f32(layers * rows, SENT, HALF), f32(1, 2)]
        args = [sums[0], sums[1], from_left, chunk, loss, loss_before]
        tile, sent, losses = call(tile_kernel, args, outs, 0, 48)
        return tile, lax.all_to_all(sent, CHIPS, 0, 0, tiled=True), losses

    def fold(*windows, token):
        both = len(windows) == 3
        strip = f32(1 + both, 2, WIN, WIN)
        return call(lambda *refs: fold_kernel(both, *refs), [*windows, token], [strip] * 3, 0, 48)

    grads, keep, send, loss_first = window_call(
        0, corners, counts, [object_field, *rims, tables[0], probe], amplitude, tables
    )
    down, up = shift(grads, "row", 1), shift(grads, "row", -1)
    part, token = reduce_chips(keep, send)
    sums = fold(grads, down, up, token=token)
    chunk, sums = lax.optimization_barrier((reduce_rows(part), sums))
    from_left, from_right = shift(sums[2], COL, 1), shift(sums[0], COL, -1)
    tile_first, mine, _ = finish_tile(sums, from_left, chunk, loss_first, loss_first)
    patches = call(
        patch_kernel,
        [corners, object_field, *rims, *sums, from_left, from_right],
        [f32(CAP, 2, WIN, WIN)] * 2,
        1,
    )

    mine, patches = lax.optimization_barrier((mine, patches))

    grads, keep, send, probe_mid, rate_first, loss_second = window_call(
        1, corners, counts, [mine, swap(mine), probe, *patches, tables[0]], amplitude, tables
    )
    down = shift(grads, "row", 1)
    part, token = reduce_chips(keep, send)
    sums = fold(grads, down, token=token)
    chunk, sums = lax.optimization_barrier((reduce_rows(part), sums))
    from_left = shift(sums[2], COL, 1)
    tile_second, mine, losses = finish_tile(sums, from_left, chunk, loss_second, loss_first)
    object_out, probe_out = final_call(
        rate_first, [mine, swap(mine), probe_mid, object_field, tile_first, tile_second]
    )
    losses = losses.reshape(1, 1, 2).transpose(2, 0, 1)
    return (object_out, probe_out.reshape(MODES, 2, WIN, WIN), losses)


def solution(mesh):
    rows, cols = mesh.shape["row"], mesh.shape["col"]
    fine = Mesh(mesh.devices.reshape(rows, cols // 2, 2), ("row", "layer", "core"))
    in_specs = (
        P(None, "row", COL),
        P(),
        P(None, "row", COL, None, None),
        P(None, "row", COL),
        P(None, "row", COL, None, None, None),
    )
    out_specs = (P(None, "row", COL), P(), P(None, "row", COL))
    return jax.shard_map(body, mesh=fine, in_specs=in_specs, out_specs=out_specs, check_vma=False)
```

```python
import math

import jax
import jax.numpy as jnp
import numpy as np
from jax import lax
from jax.experimental import pallas as pl
from jax.experimental.pallas import tpu as pltpu
from jax.sharding import Mesh
from jax.sharding import PartitionSpec as P

WIN = 256
HALF = 128
MODES = 3
CAP = 2
AREA = float(WIN * WIN)
CHUNK = 24
INFO = 8
SENT = 32
MEGA = 1024 * 1024
F32 = jnp.float32
SMEM = pl.BlockSpec(memory_space=pltpu.SMEM)
VMEM = pl.BlockSpec(memory_space=pltpu.VMEM)
ANY = pl.BlockSpec(memory_space=pl.ANY)


def f32(*shape):
    return jax.ShapeDtypeStruct(shape, F32)


def split_bf16(value):
    high = value.astype(jnp.bfloat16)
    low = (value - high.astype(F32)).astype(jnp.bfloat16)
    return high, low


def transform_tables():
    freq = np.arange(HALF)[:, None]
    pixel = np.arange(HALF)[None, :]
    tables = []
    for odd in (0, 1):
        angle = -2.0 * math.pi * (((2 * freq + odd) * pixel) % WIN) / WIN
        cos, sin = np.cos(angle) / math.sqrt(WIN), np.sin(angle) / math.sqrt(WIN)
        tables.append(np.block([[cos, -sin], [sin, cos]]).astype(np.float32))
    tables = np.stack([tables[0], tables[1], tables[0].T, tables[1].T])
    high = tables.astype(jnp.bfloat16)
    low = (tables - high.astype(np.float32)).astype(jnp.bfloat16)
    order = np.concatenate([np.arange(0, WIN, 2), np.arange(1, WIN, 2)])
    shuffle = np.zeros((WIN, WIN), np.float32)
    shuffle[np.arange(WIN), order] = 1.0
    return np.stack([high, low], axis=1), np.stack([shuffle, shuffle.T]).astype(jnp.bfloat16)


def product(left, right):
    return jnp.dot(left, right, preferred_element_type=F32)


def left_apply(table_ref, index, data):
    high, low = split_bf16(data)
    table = jnp.concatenate([table_ref[index, 0], table_ref[index, 0], table_ref[index, 1]], axis=1)
    return product(table, jnp.concatenate([high, low, high], axis=0))


def right_apply(lhs, odd, table_ref, index):
    both, high = lhs[odd], lhs[odd, :, :WIN]
    table = jnp.concatenate([table_ref[index, 0], table_ref[index, 0], table_ref[index, 1]], axis=0)
    return product(jnp.concatenate([both, high], axis=1), table)


def row_place(shape=(WIN, WIN)):
    return lax.broadcasted_iota(jnp.int32, shape, 0)


def col_place(shape=(WIN, WIN)):
    return lax.broadcasted_iota(jnp.int32, shape, 1)


def corner_of(corner_ref, iteration, slot):
    row, col = corner_ref[iteration, slot, 0], corner_ref[iteration, slot, 1]
    return lax.rem(row, WIN), lax.rem(col, WIN), lax.rem(lax.div(col, WIN), 2)


def cut(corner, upper, lower):
    row, col, block = corner
    first = row_place() >= row
    blocks = [jnp.where(first, above, below) for above, below in zip(upper, lower)]
    left = jnp.where(block == 0, blocks[0], blocks[1])
    right = jnp.where(block == 0, blocks[1], blocks[2])
    value = jnp.where(col_place() >= col, left, right)
    value = pltpu.roll(value, lax.rem(WIN - row, WIN), 0)
    return pltpu.roll(value, lax.rem(WIN - col, WIN), 1)


def rate_of(mine, other):
    total = jnp.sum(mine[:, CHUNK:], axis=0) + jnp.sum(other[:, CHUNK:], axis=0)
    return total[0:1] / (total[1:2] + 1e-06)


def gathered_plane(half, index):
    pieces, row, end = [], index * WIN, (index + 1) * WIN
    while row < end:
        chunk, offset = divmod(row, CHUNK)
        size = min(CHUNK - offset, end - row)
        pieces.append(half[chunk, offset : offset + size])
        row += size
    return jnp.concatenate(pieces, axis=0)


def probe_step(mine, other, core):
    planes = []
    for plane in range(2 * MODES):
        sides = []
        for side in range(2):
            half, index = divmod(2 * plane + side, 2 * MODES)
            own, swapped = gathered_plane(mine, index), gathered_plane(other, index)
            sides.append(jnp.where(core == half, own, swapped))
        planes.append(jnp.concatenate(sides, axis=1))
    return planes


def window_kernel(iteration, corner_ref, count_ref, *refs):
    refs = list(refs)
    core = lax.axis_index("core")
    n_big = 9 if iteration == 0 else 8
    sources, refs = refs[:n_big], refs[n_big:]
    out_grad, out_keep, out_send = refs[:3]
    refs = refs[3:]
    if iteration:
        out_mid, out_rate = refs[:2]
        refs = refs[2:]
    out_loss, obj, field, lhs, factor, total_probe, grads, sems, out_sems, probe_sems, mid_sem = refs[:11]
    direct = 5 if iteration == 0 else 0
    held = [*sources[:direct], *refs[11:]]
    fetch = [pltpu.make_async_copy(src, dst, sems.at[k]) for k, (src, dst) in enumerate(zip(sources[direct:], refs[11:]))]
    by_mode = []
    if iteration == 0:
        for mode in range(MODES):
            planes = pl.ds(2 * mode, 2)
            by_mode.append(
                pltpu.make_async_copy(sources[6].at[planes], held[6].at[planes], sems.at[len(fetch) + mode])
            )
        fetch[1:2] = by_mode
    for copy in fetch:
        copy.start()
    fetch = [None] * direct + fetch
    if iteration == 0:
        tile, below0, below1, rim, diag, tables, probe_ref, amp_ref, shuffle = held
    else:
        mine, other, probe_ref, patch, patch_grad, tables, amp_ref, shuffle = held
    for copy in fetch[direct : 5 if iteration == 0 else 3]:
        copy.wait()

    if iteration:
        rate = rate_of(mine, other)
        out_rate[...] = jnp.broadcast_to(rate, (8, HALF))
        wide = jnp.concatenate([rate, rate], axis=1)
        for plane, step in enumerate(probe_step(mine, other, core)):
            probe_ref[plane] = probe_ref[plane] - wide * step
        mid_copy = pltpu.make_async_copy(probe_ref, out_mid, mid_sem.at[0])
        mid_copy.start()

    def deliver(index):
        half, place = divmod(index, 2 * MODES)
        keep = pltpu.make_async_copy(total_probe.at[index], out_keep.at[place], probe_sems.at[index])
        send = pltpu.make_async_copy(total_probe.at[index], out_send.at[place], probe_sems.at[index])
        return half, keep, send

    losses = jnp.zeros((8, HALF), F32)
    for slot in range(CAP):
        corner = corner_of(corner_ref, iteration, slot)
        alive = (slot < count_ref[iteration]).astype(F32)
        if iteration and slot == 0:
            for copy in fetch[3:5]:
                copy.wait()
        for part in range(2):
            if iteration == 0:
                obj[part] = cut(
                    corner,
                    (tile[part, :, :WIN], tile[part, :, WIN:], rim[part]),
                    (below0[part], below1[part], diag[part]),
                )
            else:
                obj[part] = patch[slot, part] - wide * patch_grad[slot, part]

        if slot == 0:
            for copy in fetch[5 : -2 - len(by_mode)]:
                copy.wait()
        for mode in range(MODES):
            if slot == 0 and by_mode:
                by_mode[mode].wait()
            probe_re, probe_im = probe_ref[2 * mode], probe_ref[2 * mode + 1]
            exit_re = probe_re * obj[0] - probe_im * obj[1]
            exit_im = probe_re * obj[1] + probe_im * obj[0]
            half = []
            for odd in range(2):
                sign = -1.0 if odd else 1.0
                folded = jnp.concatenate(
                    [exit_re[:HALF] + sign * exit_re[HALF:], exit_im[:HALF] + sign * exit_im[HALF:]], axis=0
                )
                half.append(left_apply(tables, odd, folded))
            mid_re = jnp.concatenate([half[0][:HALF], half[1][:HALF]], axis=0)
            mid_im = jnp.concatenate([half[0][HALF:], half[1][HALF:]], axis=0)
            for odd in range(2):
                sign = -1.0 if odd else 1.0
                folded = jnp.concatenate(
                    [mid_re[:, :HALF] + sign * mid_re[:, HALF:], mid_im[:, :HALF] + sign * mid_im[:, HALF:]], axis=1
                )
                high, low = split_bf16(folded)
                rows = slice(mode * WIN, (mode + 1) * WIN)
                lhs[odd, rows, :WIN], lhs[odd, rows, WIN:] = high, low
        for odd in range(2):
            field[odd] = right_apply(lhs, odd, tables, 2 + odd)

        if slot == 0:
            fetch[-2].wait()
            fetch[-1].wait()
        amp = product(shuffle[0], amp_ref[iteration, slot]).astype(jnp.bfloat16)
        amp = product(amp, shuffle[1])
        loss = jnp.zeros((WIN, HALF), F32)
        for odd in range(2):
            total = jnp.ones((WIN, HALF), F32)
            for mode in range(MODES):
                rows = slice(mode * WIN, (mode + 1) * WIN)
                real, imag = field[odd, rows, :HALF], field[odd, rows, HALF:]
                total = total + (real * real + imag * imag)
            inverse = lax.rsqrt(total)
            measured = amp[:, odd * HALF : (odd + 1) * HALF]
            gap = total * inverse - measured
            loss = loss + gap * gap
            factor[odd] = (1.0 - measured * inverse) * (2.0 / AREA * alive)
        losses = losses + jnp.sum(loss.reshape(WIN // 8, 8, HALF), axis=0) * (alive / AREA)

        grad_re = jnp.zeros((WIN, WIN), F32)
        grad_im = jnp.zeros((WIN, WIN), F32)
        for odd in range(2):
            scale = jnp.concatenate([factor[odd], factor[odd]], axis=1)
            for mode in range(MODES):
                rows = slice(mode * WIN, (mode + 1) * WIN)
                high, low = split_bf16(field[odd, rows] * scale)
                lhs[odd, rows, :WIN], lhs[odd, rows, WIN:] = high, low
        for odd in range(2):
            field[odd] = right_apply(lhs, odd, tables, odd)
        for mode in range(MODES):
            half = [field[odd, mode * WIN : (mode + 1) * WIN] for odd in range(2)]
            mid_re = jnp.concatenate(
                [half[0][:, :HALF] + half[1][:, :HALF], half[0][:, :HALF] - half[1][:, :HALF]], axis=1
            )
            mid_im = jnp.concatenate(
                [half[0][:, HALF:] + half[1][:, HALF:], half[0][:, HALF:] - half[1][:, HALF:]], axis=1
            )
            back = []
            for odd in range(2):
                rows = slice(odd * HALF, (odd + 1) * HALF)
                back.append(left_apply(tables, 2 + odd, jnp.concatenate([mid_re[rows], mid_im[rows]], axis=0)))
            back_re = jnp.concatenate([back[0][:HALF] + back[1][:HALF], back[0][:HALF] - back[1][:HALF]], axis=0)
            back_im = jnp.concatenate([back[0][HALF:] + back[1][HALF:], back[0][HALF:] - back[1][HALF:]], axis=0)
            probe_re, probe_im = probe_ref[2 * mode], probe_ref[2 * mode + 1]
            grad_re = grad_re + (probe_re * back_re + probe_im * back_im)
            grad_im = grad_im + (probe_re * back_im - probe_im * back_re)
            terms = (obj[0] * back_re + obj[1] * back_im, obj[0] * back_im - obj[1] * back_re)
            for part in range(2):
                for side in range(2):
                    index = (2 * mode + part) * 2 + side
                    value = terms[part][:, side * HALF : (side + 1) * HALF]
                    if slot:
                        value = value + total_probe[index]
                    total_probe[index] = value
                    if slot:
                        half, keep, send = deliver(index)
                        pl.when(core == half)(keep.start)
                        pl.when(core != half)(send.start)
        for part, value in enumerate((grad_re, grad_im)):
            grads[slot, part, :WIN] = pltpu.roll(pltpu.roll(value, corner[0], 0), corner[1], 1)
            row = row_place((INFO, WIN))
            info = jnp.where(row == 0, corner[0], jnp.where(row == 1, corner[1], corner[2]))
            grads[slot, part, WIN:] = info.astype(F32)
        pltpu.make_async_copy(grads.at[slot], out_grad.at[slot], out_sems.at[slot]).start()
    out_loss[...] = losses
    for index in range(4 * MODES):
        half, keep, send = deliver(index)
        pl.when(core == half)(keep.wait)
        pl.when(core != half)(send.wait)
    for slot in range(CAP):
        pltpu.make_async_copy(grads.at[slot], out_grad.at[slot], out_sems.at[slot]).wait()
    if iteration:
        mid_copy.wait()


def call(kernel, args, out_shape, n_smem, limit=60):
    size = sum(math.prod(a.shape) * a.dtype.itemsize for a in (*args, *out_shape))
    return pl.pallas_call(
        kernel,
        out_shape=tuple(out_shape),
        in_specs=[SMEM] * n_smem + [VMEM] * (len(args) - n_smem),
        out_specs=tuple([VMEM] * len(out_shape)),
        compiler_params=pltpu.CompilerParams(vmem_limit_bytes=limit * MEGA),
        cost_estimate=pl.CostEstimate(flops=10_000_000, bytes_accessed=size, transcendentals=0),
    )(*args)


def window_call(iteration, corners, counts, data, amplitude, tables):
    outs = [f32(CAP, 2, WIN + INFO, WIN), f32(2 * MODES, WIN, HALF), f32(2 * MODES, WIN, HALF)]
    out_specs = [ANY] * 3
    if iteration:
        outs += [f32(2 * MODES, WIN, WIN), f32(8, HALF)]
        out_specs += [ANY, VMEM]
    big = [*data, amplitude, tables[1]]
    direct = 5 if iteration == 0 else 0
    return pl.pallas_call(
        lambda *refs: window_kernel(iteration, *refs),
        out_shape=(*outs, f32(8, HALF)),
        in_specs=[SMEM] * 2 + [VMEM] * direct + [ANY] * (len(big) - direct),
        out_specs=(*out_specs, VMEM),
        scratch_shapes=[
            pltpu.VMEM((2, WIN, WIN), F32),
            pltpu.VMEM((2, MODES * WIN, WIN), F32),
            pltpu.VMEM((2, MODES * WIN, 2 * WIN), jnp.bfloat16),
            pltpu.VMEM((2, WIN, HALF), F32),
            pltpu.VMEM((4 * MODES, WIN, HALF), F32),
            pltpu.VMEM((CAP, 2, WIN + INFO, WIN), F32),
            pltpu.SemaphoreType.DMA((len(big) + MODES,)),
            pltpu.SemaphoreType.DMA((CAP,)),
            pltpu.SemaphoreType.DMA((4 * MODES,)),
            pltpu.SemaphoreType.DMA((1,)),
            *[pltpu.VMEM(value.shape, value.dtype) for value in big[direct:]],
        ],
        compiler_params=pltpu.CompilerParams(vmem_limit_bytes=(60 if iteration else 48) * MEGA),
        cost_estimate=pl.CostEstimate(flops=8_000_000_000, bytes_accessed=12_000_000, transcendentals=0),
    )(corners, counts, *big)


def fold_kernel(both, *refs):
    *refs, token, out0, out1, out2 = refs
    outs = (out0, out1, out2)
    rows, cols = row_place(), col_place((1, WIN))
    masks = []
    for windows in refs:
        for slot in range(CAP):
            info = windows[slot, 0, WIN:].astype(jnp.int32)
            masks.append((rows >= info[0:1], jnp.where(cols >= info[1:2], info[2:3], info[2:3] + 1)))
    for part in range(2):
        top, bottom = [0.0] * 3, [0.0] * 3
        for which, windows in enumerate(refs):
            for slot in range(CAP):
                first, target = masks[which * CAP + slot]
                window = windows[slot, part, :WIN]
                upper = jnp.where(first, window, 0.0) if which != 1 else None
                lower = jnp.where(first, 0.0, window) if which != 2 else None
                for index in range(3):
                    here = target == index
                    if which == 0:
                        top[index] += jnp.where(here, upper, 0.0)
                        if both:
                            bottom[index] += jnp.where(here, lower, 0.0)
                    elif which == 1:
                        top[index] += jnp.where(here, lower, 0.0)
                    else:
                        bottom[index] += jnp.where(here, upper, 0.0)
        for index in range(3):
            outs[index][0, part] = top[index]
            if both:
                outs[index][1, part] = bottom[index]
    outs[0][0, 0, :8, :HALF] = outs[0][0, 0, :8, :HALF] + token[...]


def add_kernel(keep, other, out):
    out[...] = keep[...] + other[...]


def sum_kernel(parts, out, out_token):
    out[...] = jnp.sum(parts[...], axis=0)
    out_token[...] = jnp.zeros_like(out_token)


def tile_kernel(block0, block1, from_left, parts, loss, loss_before, out_tile, out_sent, out_loss):
    chunk = jnp.sum(parts[...], axis=0)
    square = sum(chunk[k : k + 8] * chunk[k : k + 8] for k in range(0, CHUNK, 8))
    for part in range(2):
        values = (block0[0, part] + from_left[0, part], block1[0, part])
        for index, value in enumerate(values):
            out_tile[part, :, index * WIN : (index + 1) * WIN] = value
            pieces = jnp.sum((value * value).reshape(WIN // 8, 8, WIN), axis=0)
            square = square + (pieces[:, :HALF] + pieces[:, HALF:])
    loss = jnp.sum(loss[...])
    out_loss[...] = jnp.where(col_place((1, 2)) == 0, jnp.sum(loss_before[...]), loss)
    scalars = jnp.where(row_place((SENT - CHUNK, HALF)) == 0, loss, jnp.sum(square))
    value = jnp.concatenate([chunk, scalars], axis=0)
    for index in range(out_sent.shape[0]):
        out_sent[index] = value


def patch_kernel(corner_ref, tile, below0, below1, rim, diag, block0, block1, block2, left, right, out_obj, out_grad):
    for part in range(2):
        upper = (tile[part, :, :WIN], tile[part, :, WIN:], rim[part])
        lower = (below0[part], below1[part], diag[part])
        grad = [
            (block0[k, part] + left[k, part], block1[k, part], block2[k, part] + right[k, part]) for k in range(2)
        ]
        for slot in range(CAP):
            corner = corner_of(corner_ref, 1, slot)
            out_obj[slot, part] = cut(corner, upper, lower)
            out_grad[slot, part] = cut(corner, grad[0], grad[1])


def final_kernel(rate_first, *refs):
    sources, (out_tile, out_probe) = refs[:6], refs[6:8]
    held, (new_tile, new_probe), sems, tile_sems, probe_sems = refs[8:14], refs[14:16], *refs[16:]
    fetch = [pltpu.make_async_copy(src, dst, sems.at[k]) for k, (src, dst) in enumerate(zip(sources, held))]
    for copy in fetch:
        copy.start()
    mine, other, probe, tile, grad_first, grad_second = held
    core = lax.axis_index("core")
    for copy in fetch[:3]:
        copy.wait()
    rate = rate_of(mine, other)
    wide = jnp.concatenate([rate, rate], axis=1)
    back = []
    for plane, step in enumerate(probe_step(mine, other, core)):
        new_probe[plane] = probe[plane] - wide * step
        back.append(pltpu.make_async_copy(new_probe.at[plane], out_probe.at[plane], probe_sems.at[plane]))
        back[-1].start()
    for copy in fetch[3:]:
        copy.wait()
    first = jnp.concatenate([rate_first[0:1]] * 4, axis=1)
    second = jnp.concatenate([rate] * 4, axis=1)
    for part in range(2):
        new_tile[part] = (tile[part] - first * grad_first[part]) - second * grad_second[part]
        back.append(pltpu.make_async_copy(new_tile.at[part], out_tile.at[part], tile_sems.at[part]))
        back[-1].start()
    for copy in back:
        copy.wait()


def final_call(rate_first, data):
    outs = (f32(2, WIN, 2 * WIN), f32(2 * MODES, WIN, WIN))
    return pl.pallas_call(
        final_kernel,
        out_shape=outs,
        in_specs=[VMEM] + [ANY] * len(data),
        out_specs=(ANY, ANY),
        scratch_shapes=[
            *[pltpu.VMEM(value.shape, value.dtype) for value in (*data, *outs)],
            pltpu.SemaphoreType.DMA((len(data),)),
            pltpu.SemaphoreType.DMA((2,)),
            pltpu.SemaphoreType.DMA((2 * MODES,)),
        ],
        compiler_params=pltpu.CompilerParams(vmem_limit_bytes=48 * MEGA),
        cost_estimate=pl.CostEstimate(flops=10_000_000, bytes_accessed=9_000_000, transcendentals=0),
    )(rate_first, *data)


def shift(value, axis, steps):
    count = math.prod(lax.axis_size(a) for a in axis) if isinstance(axis, tuple) else lax.axis_size(axis)
    first, last = max(0, -steps), min(count, count - steps)
    return lax.ppermute(value, axis, [(source, source + steps) for source in range(first, last)])


COL = ("layer", "core")
CHIPS = ("layer", "row")


def body(object_field, probe, corners, counts, amplitude):
    layers, rows = lax.axis_size("layer"), lax.axis_size("row")
    tables = [jnp.asarray(table) for table in transform_tables()]
    probe = probe.reshape(2 * MODES, WIN, WIN)
    corners, counts = corners[:, 0, 0], counts[:, 0, 0]
    amplitude = amplitude[:, 0, 0]

    first_cols = object_field[:, :, :WIN]
    below0 = shift(first_cols, "row", -1)
    rim = shift(first_cols, COL, -1)
    first_cols, again = lax.optimization_barrier((first_cols, object_field))
    below1 = shift(again[:, :, WIN:], "row", -1)
    diag = shift(below0, COL, -1)
    rims = (below0, below1, rim, diag)

    def swap(value):
        return lax.ppermute(value, "core", [(0, 1), (1, 0)])

    def reduce_chips(keep, send):
        (value,) = call(add_kernel, [keep, swap(send)], [f32(*keep.shape)], 0, 48)
        parts = lax.all_to_all(value.reshape(layers, rows * CHUNK, HALF), "layer", 0, 0, tiled=True)
        return call(sum_kernel, [parts], [f32(rows * CHUNK, HALF), f32(8, HALF)], 0, 48)

    def reduce_rows(part):
        return lax.all_to_all(part.reshape(rows, CHUNK, HALF), "row", 0, 0, tiled=True)

    def finish_tile(sums, from_left, chunk, loss, loss_before):
        outs = [f32(2, WIN, 2 * WIN), f32(layers * rows, SENT, HALF), f32(1, 2)]
        args = [sums[0], sums[1], from_left, chunk, loss, loss_before]
        tile, sent, losses = call(tile_kernel, args, outs, 0, 48)
        return tile, lax.all_to_all(sent, CHIPS, 0, 0, tiled=True), losses

    def fold(*windows, token):
        both = len(windows) == 3
        strip = f32(1 + both, 2, WIN, WIN)
        return call(lambda *refs: fold_kernel(both, *refs), [*windows, token], [strip] * 3, 0, 48)

    grads, keep, send, loss_first = window_call(
        0, corners, counts, [object_field, *rims, tables[0], probe], amplitude, tables
    )
    down, up = shift(grads, "row", 1), shift(grads, "row", -1)
    part, token = reduce_chips(keep, send)
    sums = fold(grads, down, up, token=token)
    chunk, sums = lax.optimization_barrier((reduce_rows(part), sums))
    from_left, from_right = shift(sums[2], COL, 1), shift(sums[0], COL, -1)
    tile_first, mine, _ = finish_tile(sums, from_left, chunk, loss_first, loss_first)
    patches = call(
        patch_kernel,
        [corners, object_field, *rims, *sums, from_left, from_right],
        [f32(CAP, 2, WIN, WIN)] * 2,
        1,
    )

    mine, patches = lax.optimization_barrier((mine, patches))

    grads, keep, send, probe_mid, rate_first, loss_second = window_call(
        1, corners, counts, [mine, swap(mine), probe, *patches, tables[0]], amplitude, tables
    )
    down = shift(grads, "row", 1)
    part, token = reduce_chips(keep, send)
    sums = fold(grads, down, token=token)
    chunk, sums = lax.optimization_barrier((reduce_rows(part), sums))
    from_left = shift(sums[2], COL, 1)
    tile_second, mine, losses = finish_tile(sums, from_left, chunk, loss_second, loss_first)
    object_out, probe_out = final_call(
        rate_first, [mine, swap(mine), probe_mid, object_field, tile_first, tile_second]
    )
    losses = losses.reshape(1, 1, 2).transpose(2, 0, 1)
    return (object_out, probe_out.reshape(MODES, 2, WIN, WIN), losses)


def solution(mesh):
    rows, cols = mesh.shape["row"], mesh.shape["col"]
    fine = Mesh(mesh.devices.reshape(rows, cols // 2, 2), ("row", "layer", "core"))
    in_specs = (
        P(None, "row", COL),
        P(),
        P(None, "row", COL, None, None),
        P(None, "row", COL),
        P(None, "row", COL, None, None, None),
    )
    out_specs = (P(None, "row", COL), P(), P(None, "row", COL))
    return jax.shard_map(body, mesh=fine, in_specs=in_specs, out_specs=out_specs, check_vma=False)
```

```python
import math

import jax
import jax.numpy as jnp
import numpy as np
from jax import lax
from jax.experimental import pallas as pl
from jax.experimental.pallas import tpu as pltpu
from jax.sharding import Mesh
from jax.sharding import PartitionSpec as P

WIN = 256
HALF = 128
MODES = 3
CAP = 2
AREA = float(WIN * WIN)
CHUNK = 24
INFO = 8
SENT = 32
MEGA = 1024 * 1024
F32 = jnp.float32
SMEM = pl.BlockSpec(memory_space=pltpu.SMEM)
VMEM = pl.BlockSpec(memory_space=pltpu.VMEM)
ANY = pl.BlockSpec(memory_space=pl.ANY)


def f32(*shape):
    return jax.ShapeDtypeStruct(shape, F32)


def split_bf16(value):
    high = value.astype(jnp.bfloat16)
    low = (value - high.astype(F32)).astype(jnp.bfloat16)
    return high, low


def transform_tables():
    freq = np.arange(HALF)[:, None]
    pixel = np.arange(HALF)[None, :]
    tables = []
    for odd in (0, 1):
        angle = -2.0 * math.pi * (((2 * freq + odd) * pixel) % WIN) / WIN
        cos, sin = np.cos(angle) / math.sqrt(WIN), np.sin(angle) / math.sqrt(WIN)
        tables.append(np.block([[cos, -sin], [sin, cos]]).astype(np.float32))
    tables = np.stack([tables[0], tables[1], tables[0].T, tables[1].T])
    high = tables.astype(jnp.bfloat16)
    low = (tables - high.astype(np.float32)).astype(jnp.bfloat16)
    order = np.concatenate([np.arange(0, WIN, 2), np.arange(1, WIN, 2)])
    shuffle = np.zeros((WIN, WIN), np.float32)
    shuffle[np.arange(WIN), order] = 1.0
    return np.stack([high, low], axis=1), np.stack([shuffle, shuffle.T]).astype(jnp.bfloat16)


def product(left, right):
    return jnp.dot(left, right, preferred_element_type=F32)


def left_apply(table_ref, index, data):
    high, low = split_bf16(data)
    table = jnp.concatenate([table_ref[index, 0], table_ref[index, 0], table_ref[index, 1]], axis=1)
    return product(table, jnp.concatenate([high, low, high], axis=0))


def right_apply(lhs, odd, table_ref, index):
    both, high = lhs[odd], lhs[odd, :, :WIN]
    table = jnp.concatenate([table_ref[index, 0], table_ref[index, 0], table_ref[index, 1]], axis=0)
    return product(jnp.concatenate([both, high], axis=1), table)


def row_place(shape=(WIN, WIN)):
    return lax.broadcasted_iota(jnp.int32, shape, 0)


def col_place(shape=(WIN, WIN)):
    return lax.broadcasted_iota(jnp.int32, shape, 1)


def corner_of(corner_ref, iteration, slot):
    row, col = corner_ref[iteration, slot, 0], corner_ref[iteration, slot, 1]
    return lax.rem(row, WIN), lax.rem(col, WIN), lax.rem(lax.div(col, WIN), 2)


def cut(corner, upper, lower):
    row, col, block = corner
    first = row_place() >= row
    blocks = [jnp.where(first, above, below) for above, below in zip(upper, lower)]
    left = jnp.where(block == 0, blocks[0], blocks[1])
    right = jnp.where(block == 0, blocks[1], blocks[2])
    value = jnp.where(col_place() >= col, left, right)
    value = pltpu.roll(value, lax.rem(WIN - row, WIN), 0)
    return pltpu.roll(value, lax.rem(WIN - col, WIN), 1)


def rate_of(mine, other):
    total = jnp.sum(mine[:, CHUNK:], axis=0) + jnp.sum(other[:, CHUNK:], axis=0)
    return total[0:1] / (total[1:2] + 1e-06)


def gathered_plane(half, index):
    pieces, row, end = [], index * WIN, (index + 1) * WIN
    while row < end:
        chunk, offset = divmod(row, CHUNK)
        size = min(CHUNK - offset, end - row)
        pieces.append(half[chunk, offset : offset + size])
        row += size
    return jnp.concatenate(pieces, axis=0)


def probe_step(mine, other, core):
    planes = []
    for plane in range(2 * MODES):
        sides = []
        for side in range(2):
            half, index = divmod(2 * plane + side, 2 * MODES)
            own, swapped = gathered_plane(mine, index), gathered_plane(other, index)
            sides.append(jnp.where(core == half, own, swapped))
        planes.append(jnp.concatenate(sides, axis=1))
    return planes


def window_kernel(iteration, corner_ref, count_ref, *refs):
    refs = list(refs)
    core = lax.axis_index("core")
    n_big = 9 if iteration == 0 else 8
    sources, refs = refs[:n_big], refs[n_big:]
    out_grad, out_keep, out_send = refs[:3]
    refs = refs[3:]
    if iteration:
        out_mid, out_rate = refs[:2]
        refs = refs[2:]
    out_loss, obj, field, lhs, factor, total_probe, grads, sems, out_sems, probe_sems, mid_sem = refs[:11]
    held = refs[11:]
    fetch = [pltpu.make_async_copy(src, dst, sems.at[k]) for k, (src, dst) in enumerate(zip(sources, held))]
    for copy in fetch:
        copy.start()
    if iteration == 0:
        tile, below0, below1, rim, diag, tables, probe_ref, amp_ref, shuffle = held
    else:
        mine, other, probe_ref, patch, patch_grad, tables, amp_ref, shuffle = held
    for copy in fetch[: 5 if iteration == 0 else 3]:
        copy.wait()

    if iteration:
        rate = rate_of(mine, other)
        out_rate[...] = jnp.broadcast_to(rate, (8, HALF))
        wide = jnp.concatenate([rate, rate], axis=1)
        for plane, step in enumerate(probe_step(mine, other, core)):
            probe_ref[plane] = probe_ref[plane] - wide * step
        mid_copy = pltpu.make_async_copy(probe_ref, out_mid, mid_sem.at[0])
        mid_copy.start()

    def deliver(index):
        half, place = divmod(index, 2 * MODES)
        keep = pltpu.make_async_copy(total_probe.at[index], out_keep.at[place], probe_sems.at[index])
        send = pltpu.make_async_copy(total_probe.at[index], out_send.at[place], probe_sems.at[index])
        return half, keep, send

    losses = jnp.zeros((8, HALF), F32)
    for slot in range(CAP):
        corner = corner_of(corner_ref, iteration, slot)
        alive = (slot < count_ref[iteration]).astype(F32)
        if iteration and slot == 0:
            for copy in fetch[3:5]:
                copy.wait()
        for part in range(2):
            if iteration == 0:
                obj[part] = cut(
                    corner,
                    (tile[part, :, :WIN], tile[part, :, WIN:], rim[part]),
                    (below0[part], below1[part], diag[part]),
                )
            else:
                obj[part] = patch[slot, part] - wide * patch_grad[slot, part]

        if slot == 0:
            for copy in fetch[5:-2]:
                copy.wait()
        for mode in range(MODES):
            probe_re, probe_im = probe_ref[2 * mode], probe_ref[2 * mode + 1]
            exit_re = probe_re * obj[0] - probe_im * obj[1]
            exit_im = probe_re * obj[1] + probe_im * obj[0]
            half = []
            for odd in range(2):
                sign = -1.0 if odd else 1.0
                folded = jnp.concatenate(
                    [exit_re[:HALF] + sign * exit_re[HALF:], exit_im[:HALF] + sign * exit_im[HALF:]], axis=0
                )
                half.append(left_apply(tables, odd, folded))
            mid_re = jnp.concatenate([half[0][:HALF], half[1][:HALF]], axis=0)
            mid_im = jnp.concatenate([half[0][HALF:], half[1][HALF:]], axis=0)
            for odd in range(2):
                sign = -1.0 if odd else 1.0
                folded = jnp.concatenate(
                    [mid_re[:, :HALF] + sign * mid_re[:, HALF:], mid_im[:, :HALF] + sign * mid_im[:, HALF:]], axis=1
                )
                high, low = split_bf16(folded)
                rows = slice(mode * WIN, (mode + 1) * WIN)
                lhs[odd, rows, :WIN], lhs[odd, rows, WIN:] = high, low
        for odd in range(2):
            field[odd] = right_apply(lhs, odd, tables, 2 + odd)

        if slot == 0:
            fetch[-2].wait()
            fetch[-1].wait()
        amp = product(shuffle[0], amp_ref[iteration, slot]).astype(jnp.bfloat16)
        amp = product(amp, shuffle[1])
        loss = jnp.zeros((WIN, HALF), F32)
        for odd in range(2):
            total = jnp.ones((WIN, HALF), F32)
            for mode in range(MODES):
                rows = slice(mode * WIN, (mode + 1) * WIN)
                real, imag = field[odd, rows, :HALF], field[odd, rows, HALF:]
                total = total + (real * real + imag * imag)
            inverse = lax.rsqrt(total)
            measured = amp[:, odd * HALF : (odd + 1) * HALF]
            gap = total * inverse - measured
            loss = loss + gap * gap
            factor[odd] = (1.0 - measured * inverse) * (2.0 / AREA * alive)
        losses = losses + jnp.sum(loss.reshape(WIN // 8, 8, HALF), axis=0) * (alive / AREA)

        grad_re = jnp.zeros((WIN, WIN), F32)
        grad_im = jnp.zeros((WIN, WIN), F32)
        for odd in range(2):
            scale = jnp.concatenate([factor[odd], factor[odd]], axis=1)
            for mode in range(MODES):
                rows = slice(mode * WIN, (mode + 1) * WIN)
                high, low = split_bf16(field[odd, rows] * scale)
                lhs[odd, rows, :WIN], lhs[odd, rows, WIN:] = high, low
        for odd in range(2):
            field[odd] = right_apply(lhs, odd, tables, odd)
        for mode in range(MODES):
            half = [field[odd, mode * WIN : (mode + 1) * WIN] for odd in range(2)]
            mid_re = jnp.concatenate(
                [half[0][:, :HALF] + half[1][:, :HALF], half[0][:, :HALF] - half[1][:, :HALF]], axis=1
            )
            mid_im = jnp.concatenate(
                [half[0][:, HALF:] + half[1][:, HALF:], half[0][:, HALF:] - half[1][:, HALF:]], axis=1
            )
            back = []
            for odd in range(2):
                rows = slice(odd * HALF, (odd + 1) * HALF)
                back.append(left_apply(tables, 2 + odd, jnp.concatenate([mid_re[rows], mid_im[rows]], axis=0)))
            back_re = jnp.concatenate([back[0][:HALF] + back[1][:HALF], back[0][:HALF] - back[1][:HALF]], axis=0)
            back_im = jnp.concatenate([back[0][HALF:] + back[1][HALF:], back[0][HALF:] - back[1][HALF:]], axis=0)
            probe_re, probe_im = probe_ref[2 * mode], probe_ref[2 * mode + 1]
            grad_re = grad_re + (probe_re * back_re + probe_im * back_im)
            grad_im = grad_im + (probe_re * back_im - probe_im * back_re)
            terms = (obj[0] * back_re + obj[1] * back_im, obj[0] * back_im - obj[1] * back_re)
            for part in range(2):
                for side in range(2):
                    index = (2 * mode + part) * 2 + side
                    value = terms[part][:, side * HALF : (side + 1) * HALF]
                    if slot:
                        value = value + total_probe[index]
                    total_probe[index] = value
                    if slot:
                        half, keep, send = deliver(index)
                        pl.when(core == half)(keep.start)
                        pl.when(core != half)(send.start)
        for part, value in enumerate((grad_re, grad_im)):
            grads[slot, part, :WIN] = pltpu.roll(pltpu.roll(value, corner[0], 0), corner[1], 1)
            row = row_place((INFO, WIN))
            info = jnp.where(row == 0, corner[0], jnp.where(row == 1, corner[1], corner[2]))
            grads[slot, part, WIN:] = info.astype(F32)
        pltpu.make_async_copy(grads.at[slot], out_grad.at[slot], out_sems.at[slot]).start()
    out_loss[...] = losses
    for index in range(4 * MODES):
        half, keep, send = deliver(index)
        pl.when(core == half)(keep.wait)
        pl.when(core != half)(send.wait)
    for slot in range(CAP):
        pltpu.make_async_copy(grads.at[slot], out_grad.at[slot], out_sems.at[slot]).wait()
    if iteration:
        mid_copy.wait()


def call(kernel, args, out_shape, n_smem, limit=60):
    size = sum(math.prod(a.shape) * a.dtype.itemsize for a in (*args, *out_shape))
    return pl.pallas_call(
        kernel,
        out_shape=tuple(out_shape),
        in_specs=[SMEM] * n_smem + [VMEM] * (len(args) - n_smem),
        out_specs=tuple([VMEM] * len(out_shape)),
        compiler_params=pltpu.CompilerParams(vmem_limit_bytes=limit * MEGA),
        cost_estimate=pl.CostEstimate(flops=10_000_000, bytes_accessed=size, transcendentals=0),
    )(*args)


def window_call(iteration, corners, counts, data, amplitude, tables):
    outs = [f32(CAP, 2, WIN + INFO, WIN), f32(2 * MODES, WIN, HALF), f32(2 * MODES, WIN, HALF)]
    out_specs = [ANY] * 3
    if iteration:
        outs += [f32(2 * MODES, WIN, WIN), f32(8, HALF)]
        out_specs += [ANY, VMEM]
    big = [*data, amplitude, tables[1]]
    return pl.pallas_call(
        lambda *refs: window_kernel(iteration, *refs),
        out_shape=(*outs, f32(8, HALF)),
        in_specs=[SMEM] * 2 + [ANY] * len(big),
        out_specs=(*out_specs, VMEM),
        scratch_shapes=[
            pltpu.VMEM((2, WIN, WIN), F32),
            pltpu.VMEM((2, MODES * WIN, WIN), F32),
            pltpu.VMEM((2, MODES * WIN, 2 * WIN), jnp.bfloat16),
            pltpu.VMEM((2, WIN, HALF), F32),
            pltpu.VMEM((4 * MODES, WIN, HALF), F32),
            pltpu.VMEM((CAP, 2, WIN + INFO, WIN), F32),
            pltpu.SemaphoreType.DMA((len(big),)),
            pltpu.SemaphoreType.DMA((CAP,)),
            pltpu.SemaphoreType.DMA((4 * MODES,)),
            pltpu.SemaphoreType.DMA((1,)),
            *[pltpu.VMEM(value.shape, value.dtype) for value in big],
        ],
        compiler_params=pltpu.CompilerParams(vmem_limit_bytes=60 * MEGA),
        cost_estimate=pl.CostEstimate(flops=8_000_000_000, bytes_accessed=12_000_000, transcendentals=0),
    )(corners, counts, *big)


def fold_kernel(both, *refs):
    *refs, token, out0, out1, out2 = refs
    outs = (out0, out1, out2)
    rows, cols = row_place(), col_place((1, WIN))
    masks = []
    for windows in refs:
        for slot in range(CAP):
            info = windows[slot, 0, WIN:].astype(jnp.int32)
            masks.append((rows >= info[0:1], jnp.where(cols >= info[1:2], info[2:3], info[2:3] + 1)))
    for part in range(2):
        top, bottom = [0.0] * 3, [0.0] * 3
        for which, windows in enumerate(refs):
            for slot in range(CAP):
                first, target = masks[which * CAP + slot]
                window = windows[slot, part, :WIN]
                upper = jnp.where(first, window, 0.0) if which != 1 else None
                lower = jnp.where(first, 0.0, window) if which != 2 else None
                for index in range(3):
                    here = target == index
                    if which == 0:
                        top[index] += jnp.where(here, upper, 0.0)
                        if both:
                            bottom[index] += jnp.where(here, lower, 0.0)
                    elif which == 1:
                        top[index] += jnp.where(here, lower, 0.0)
                    else:
                        bottom[index] += jnp.where(here, upper, 0.0)
        for index in range(3):
            outs[index][0, part] = top[index]
            if both:
                outs[index][1, part] = bottom[index]
    outs[0][0, 0, :8, :HALF] = outs[0][0, 0, :8, :HALF] + token[...]


def add_kernel(keep, other, out):
    out[...] = keep[...] + other[...]


def sum_kernel(parts, out, out_token):
    out[...] = jnp.sum(parts[...], axis=0)
    out_token[...] = jnp.zeros_like(out_token)


def tile_kernel(block0, block1, from_left, parts, loss, loss_before, out_tile, out_sent, out_loss):
    chunk = jnp.sum(parts[...], axis=0)
    square = sum(chunk[k : k + 8] * chunk[k : k + 8] for k in range(0, CHUNK, 8))
    for part in range(2):
        values = (block0[0, part] + from_left[0, part], block1[0, part])
        for index, value in enumerate(values):
            out_tile[part, :, index * WIN : (index + 1) * WIN] = value
            pieces = jnp.sum((value * value).reshape(WIN // 8, 8, WIN), axis=0)
            square = square + (pieces[:, :HALF] + pieces[:, HALF:])
    loss = jnp.sum(loss[...])
    out_loss[...] = jnp.where(col_place((1, 2)) == 0, jnp.sum(loss_before[...]), loss)
    scalars = jnp.where(row_place((SENT - CHUNK, HALF)) == 0, loss, jnp.sum(square))
    value = jnp.concatenate([chunk, scalars], axis=0)
    for index in range(out_sent.shape[0]):
        out_sent[index] = value


def patch_kernel(corner_ref, tile, below0, below1, rim, diag, block0, block1, block2, left, right, out_obj, out_grad):
    for part in range(2):
        upper = (tile[part, :, :WIN], tile[part, :, WIN:], rim[part])
        lower = (below0[part], below1[part], diag[part])
        grad = [
            (block0[k, part] + left[k, part], block1[k, part], block2[k, part] + right[k, part]) for k in range(2)
        ]
        for slot in range(CAP):
            corner = corner_of(corner_ref, 1, slot)
            out_obj[slot, part] = cut(corner, upper, lower)
            out_grad[slot, part] = cut(corner, grad[0], grad[1])


def final_kernel(rate_first, *refs):
    sources, (out_tile, out_probe) = refs[:6], refs[6:8]
    held, (new_tile, new_probe), sems, tile_sems, probe_sems = refs[8:14], refs[14:16], *refs[16:]
    fetch = [pltpu.make_async_copy(src, dst, sems.at[k]) for k, (src, dst) in enumerate(zip(sources, held))]
    for copy in fetch:
        copy.start()
    mine, other, probe, tile, grad_first, grad_second = held
    core = lax.axis_index("core")
    for copy in fetch[:3]:
        copy.wait()
    rate = rate_of(mine, other)
    wide = jnp.concatenate([rate, rate], axis=1)
    back = []
    for plane, step in enumerate(probe_step(mine, other, core)):
        new_probe[plane] = probe[plane] - wide * step
        back.append(pltpu.make_async_copy(new_probe.at[plane], out_probe.at[plane], probe_sems.at[plane]))
        back[-1].start()
    for copy in fetch[3:]:
        copy.wait()
    first = jnp.concatenate([rate_first[0:1]] * 4, axis=1)
    second = jnp.concatenate([rate] * 4, axis=1)
    for part in range(2):
        new_tile[part] = (tile[part] - first * grad_first[part]) - second * grad_second[part]
        back.append(pltpu.make_async_copy(new_tile.at[part], out_tile.at[part], tile_sems.at[part]))
        back[-1].start()
    for copy in back:
        copy.wait()


def final_call(rate_first, data):
    outs = (f32(2, WIN, 2 * WIN), f32(2 * MODES, WIN, WIN))
    return pl.pallas_call(
        final_kernel,
        out_shape=outs,
        in_specs=[VMEM] + [ANY] * len(data),
        out_specs=(ANY, ANY),
        scratch_shapes=[
            *[pltpu.VMEM(value.shape, value.dtype) for value in (*data, *outs)],
            pltpu.SemaphoreType.DMA((len(data),)),
            pltpu.SemaphoreType.DMA((2,)),
            pltpu.SemaphoreType.DMA((2 * MODES,)),
        ],
        compiler_params=pltpu.CompilerParams(vmem_limit_bytes=48 * MEGA),
        cost_estimate=pl.CostEstimate(flops=10_000_000, bytes_accessed=9_000_000, transcendentals=0),
    )(rate_first, *data)


def shift(value, axis, steps):
    count = math.prod(lax.axis_size(a) for a in axis) if isinstance(axis, tuple) else lax.axis_size(axis)
    first, last = max(0, -steps), min(count, count - steps)
    return lax.ppermute(value, axis, [(source, source + steps) for source in range(first, last)])


COL = ("layer", "core")
CHIPS = ("layer", "row")


def body(object_field, probe, corners, counts, amplitude):
    layers, rows = lax.axis_size("layer"), lax.axis_size("row")
    tables = [jnp.asarray(table) for table in transform_tables()]
    probe = probe.reshape(2 * MODES, WIN, WIN)
    corners, counts = corners[:, 0, 0], counts[:, 0, 0]
    amplitude = amplitude[:, 0, 0]

    first_cols = object_field[:, :, :WIN]
    below0 = shift(first_cols, "row", -1)
    rim = shift(first_cols, COL, -1)
    first_cols, again = lax.optimization_barrier((first_cols, object_field))
    below1 = shift(again[:, :, WIN:], "row", -1)
    diag = shift(below0, COL, -1)
    rims = (below0, below1, rim, diag)

    def swap(value):
        return lax.ppermute(value, "core", [(0, 1), (1, 0)])

    def reduce_chips(keep, send):
        (value,) = call(add_kernel, [keep, swap(send)], [f32(*keep.shape)], 0, 48)
        parts = lax.all_to_all(value.reshape(layers, rows * CHUNK, HALF), "layer", 0, 0, tiled=True)
        return call(sum_kernel, [parts], [f32(rows * CHUNK, HALF), f32(8, HALF)], 0, 48)

    def reduce_rows(part):
        return lax.all_to_all(part.reshape(rows, CHUNK, HALF), "row", 0, 0, tiled=True)

    def finish_tile(sums, from_left, chunk, loss, loss_before):
        outs = [f32(2, WIN, 2 * WIN), f32(layers * rows, SENT, HALF), f32(1, 2)]
        args = [sums[0], sums[1], from_left, chunk, loss, loss_before]
        tile, sent, losses = call(tile_kernel, args, outs, 0, 48)
        return tile, lax.all_to_all(sent, CHIPS, 0, 0, tiled=True), losses

    def fold(*windows, token):
        both = len(windows) == 3
        strip = f32(1 + both, 2, WIN, WIN)
        return call(lambda *refs: fold_kernel(both, *refs), [*windows, token], [strip] * 3, 0, 48)

    grads, keep, send, loss_first = window_call(
        0, corners, counts, [object_field, *rims, tables[0], probe], amplitude, tables
    )
    down, up = shift(grads, "row", 1), shift(grads, "row", -1)
    part, token = reduce_chips(keep, send)
    sums = fold(grads, down, up, token=token)
    chunk, sums = lax.optimization_barrier((reduce_rows(part), sums))
    from_left, from_right = shift(sums[2], COL, 1), shift(sums[0], COL, -1)
    tile_first, mine, _ = finish_tile(sums, from_left, chunk, loss_first, loss_first)
    patches = call(
        patch_kernel,
        [corners, object_field, *rims, *sums, from_left, from_right],
        [f32(CAP, 2, WIN, WIN)] * 2,
        1,
    )

    mine, patches = lax.optimization_barrier((mine, patches))

    grads, keep, send, probe_mid, rate_first, loss_second = window_call(
        1, corners, counts, [mine, swap(mine), probe, *patches, tables[0]], amplitude, tables
    )
    down = shift(grads, "row", 1)
    part, token = reduce_chips(keep, send)
    sums = fold(grads, down, token=token)
    chunk, sums = lax.optimization_barrier((reduce_rows(part), sums))
    from_left = shift(sums[2], COL, 1)
    tile_second, mine, losses = finish_tile(sums, from_left, chunk, loss_second, loss_first)
    object_out, probe_out = final_call(
        rate_first, [mine, swap(mine), probe_mid, object_field, tile_first, tile_second]
    )
    losses = losses.reshape(1, 1, 2).transpose(2, 0, 1)
    return (object_out, probe_out.reshape(MODES, 2, WIN, WIN), losses)


def solution(mesh):
    rows, cols = mesh.shape["row"], mesh.shape["col"]
    fine = Mesh(mesh.devices.reshape(rows, cols // 2, 2), ("row", "layer", "core"))
    in_specs = (
        P(None, "row", COL),
        P(),
        P(None, "row", COL, None, None),
        P(None, "row", COL),
        P(None, "row", COL, None, None, None),
    )
    out_specs = (P(None, "row", COL), P(), P(None, "row", COL))
    return jax.shard_map(body, mesh=fine, in_specs=in_specs, out_specs=out_specs, check_vma=False)
```
